128 devices in a mesh: gx: 16 (over y, x), gy: 8 (over z, core).
Axes of the slice: x: 4, y: 4, z: 4, core: 2. Of those that a mesh axis runs over, the one named last changes fastest.
Arguments:
- right_side: float32 [8, 64, 64, 256], P(None, 'gx', 'gy'), may hold values from -6 to 6
- fine_ids: int32 [64, 64, 256], P('gx', 'gy'), may hold values from 0 to 255, as said below
- coarse_diag: float32 [32, 16, 64], P('gx', 'gy'), as said below
- coarse_links: float32 [6, 32, 16, 64], P(None, 'gx', 'gy'), as said below
- coarse_ids: int32 [32, 16, 64], P('gx', 'gy'), may hold values from 0 to 2047, as said below
- coarsest_inverse: float32 [2048, 2048], P(('gx', 'gy')), as said below
Outputs:
- solution: float32 [8, 64, 64, 256], P(None, 'gx', 'gy')
The draws below stay inside these ranges and needn't reach their ends.
Inputs may be any that keep to these rules, and one draw needn't show every extreme that they name: `fine_ids`: each cell names an aggregate within its device's tile whose local coordinates differ by at most one along each dimension from (cell's local first coordinate // 2, local second coordinate // 4, third coordinate // 4). `coarse_diag`: each entry exceeds the sum of the six couplings of its aggregate. `coarse_links`: the lower coupling of an aggregate along a dimension equals the upper coupling of the aggregate below it; couplings past the grid's ends are zero. `coarse_ids`: names a coarsest unknown for each aggregate. `coarsest_inverse`: symmetric.
All inputs are finite; a program needn't handle non-finite values.
Results may differ from the reference program's by a relative error of at most 0.00013.
Values sent between devices are 32-bit elements; how exact they have to be, the bound alone decides.
No kernel may reach another device: no remote copies, remote signals or barrier semaphores. Data moves between devices by JAX's collectives and lax.ppermute only.
A program may use at most 256 MiB of HBM per device.

```python
import math
import jax
import jax.numpy as jnp
from jax import lax

RHS = 8
CX = 4
CY = 8
CZ = 256
DEGREE = 3
C2DEV = 16
AX = 2
AY = 2
AZ = 64
CAGG = 256
NX = 64
NY = 64
NAX = 32
NAY = 16
NC2 = 2048
N_GX = 16
N_GY = 8


def draw_fine_ids(key, part):
    key = jax.random.fold_in(key, 11)
    shape = (CX * N_GX, CY * N_GY, CZ)
    jitter = jax.random.randint(key, (3,) + shape, -1, 2)
    cell_x = lax.broadcasted_iota(jnp.int32, shape, 0) % CX
    cell_y = lax.broadcasted_iota(jnp.int32, shape, 1) % CY
    cell_z = lax.broadcasted_iota(jnp.int32, shape, 2)
    block_x = jnp.clip(cell_x + jitter[0], 0, CX - 1) // 2
    block_y = jnp.clip(cell_y + jitter[1], 0, CY - 1) // 4
    block_z = jnp.clip(cell_z + jitter[2], 0, CZ - 1) // 4
    return ((block_x * (CY // 4) + block_y) * (CZ // 4) + block_z).astype(jnp.int32)


def link_fields(key, low, high):
    shape = (NAX, NAY, AZ)
    keys = jax.random.split(key, 3)
    faces = [16.0, 8.0, 8.0]
    fields = []
    for axis in range(3):
        place = lax.broadcasted_iota(jnp.int32, shape, axis)
        upper = faces[axis] * jax.random.uniform(keys[axis], shape, jnp.float32, low, high)
        upper = jnp.where(place < shape[axis] - 1, upper, 0.0)
        lower = jnp.where(place >= 1, jnp.roll(upper, 1, axis=axis), 0.0)
        fields.append(lower)
        fields.append(upper)
    return jnp.stack(fields, axis=0)


def draw_coarse_links(key, part):
    links = link_fields(key, 0.5, 2.0)
    return links


def draw_coarse_diag(key, part):
    links = link_fields(key, 0.5, 2.0)
    key = jax.random.fold_in(key, 41)
    total = links[0] + links[1] + links[2] + links[3] + links[4] + links[5]
    factor = jax.random.uniform(key, (NAX, NAY, AZ), jnp.float32, 1.1, 1.5)
    return total * factor + 1.0


def draw_coarse_ids(key, part):
    key = jax.random.fold_in(key, 23)
    key_own, key_other, key_pick = jax.random.split(key, 3)
    shape = (NAX, NAY, AZ)
    total = C2DEV * N_GX * N_GY
    owner = lax.broadcasted_iota(jnp.int32, shape, 0) // AX * N_GY + lax.broadcasted_iota(jnp.int32, shape, 1) // AY
    own = owner * C2DEV + jax.random.randint(key_own, shape, 0, C2DEV)
    other = jax.random.randint(key_other, shape, 0, total)
    pick = jax.random.randint(key_pick, shape, 0, 4) == 0
    chosen = jnp.where(pick, other, own)
    chosen = chosen.at[0, 0, 0].set(0).at[NAX - 1, NAY - 1, AZ - 1].set(total - 1)
    return chosen.astype(jnp.int32)


def draw_coarsest_inverse(key, part):
    key = jax.random.fold_in(key, 29)
    key_raw = jax.random.fold_in(key, 0)
    key_diag = jax.random.fold_in(key, 2)
    count = C2DEV * N_GX * N_GY
    shape = (count, count)
    raw = jax.random.uniform(key_raw, shape, jnp.float32, -1.0, 1.0)
    mixed = 0.5 * (raw + raw.T) * (1.0 / math.sqrt(count))
    diagonal = jax.random.uniform(key_diag, (count,), jnp.float32, 1.0, 2.0)
    rows = lax.broadcasted_iota(jnp.int32, shape, 0)
    columns = lax.broadcasted_iota(jnp.int32, shape, 1)
    full = jnp.where(rows == columns, diagonal[:, None], mixed)
    return 0.04 / math.sqrt(CAGG // C2DEV) * full


def level_of(own_key, shape, cuts, low, largest):
    def one(position, shards_of):
        draws = jax.random.uniform(jax.random.fold_in(jax.random.fold_in(own_key, 6), position), (shards_of,), jnp.float32, low / len(cuts), largest / len(cuts))
        return jnp.repeat(jnp.exp(draws), shape[position] // shards_of).reshape((-1,) + (1,) * (len(shape) - position - 1))

    gain = one(*cuts[0])
    for cut in cuts[1:]:
        gain = gain * one(*cut)
    return gain


def centred(own_key, dims, deviation, bound, cuts=(), held_as=jnp.bfloat16):
    entries = deviation * jax.random.normal(own_key, dims, jnp.float32)
    if cuts:
        entries = entries * level_of(own_key, dims, cuts, -0.22, 0.18)
    return jnp.clip(entries, -bound, bound).astype(held_as)


def setup_inputs(seed: int = 0) -> dict:
    arg_keys = jax.random.split(jax.random.key(seed), 7)
    return {
        "right_side": centred(arg_keys[0], (RHS, NX, NY, CZ), 1.0, 6.0, ((1, 16), (2, 8)), jnp.float32),
        "fine_ids": draw_fine_ids(jax.random.fold_in(arg_keys[6], 71), 0),
        "coarse_diag": draw_coarse_diag(jax.random.fold_in(arg_keys[6], 71), 0),
        "coarse_links": draw_coarse_links(jax.random.fold_in(arg_keys[6], 71), 0),
        "coarse_ids": draw_coarse_ids(jax.random.fold_in(arg_keys[6], 71), 0),
        "coarsest_inverse": draw_coarsest_inverse(jax.random.fold_in(arg_keys[6], 71), 0),
    }


prolong_weight = 1.0 / 9.0
fine_low = 2.0 / 30.0
fine_high = 2.0
coarse_low = 0.19
coarse_high = 1.9


def stencil(padded):
    center = padded[:, 1:-1, 1:-1, :]
    along = jnp.pad(center, ((0, 0), (0, 0), (0, 0), (1, 1)))
    beside = padded[:, 2:, 1:-1, :] + padded[:, :-2, 1:-1, :]
    beside = beside + padded[:, 1:-1, 2:, :] + padded[:, 1:-1, :-2, :]
    beside = beside + along[:, :, :, 2:] + along[:, :, :, :-2]
    return 6.0 * center - beside


def chebyshev(operator, inverse_diag, target, guess, low, high):
    theta = (high + low) / 2.0
    delta = (high - low) / 2.0
    sigma = theta / delta
    rho_old = 1.0 / sigma
    if guess is None:
        residual = target
        iterate = jnp.zeros_like(target)
    else:
        residual = target - operator(guess)
        iterate = guess
    update = inverse_diag * residual / theta
    iterate = iterate + update
    for step in range(DEGREE - 1):
        residual = residual - operator(update)
        rho_new = 1.0 / (2.0 * sigma - rho_old)
        update = rho_new * rho_old * update + (2.0 * rho_new / delta) * inverse_diag * residual
        iterate = iterate + update
        rho_old = rho_new
    return iterate


def fine_apply(field):
    return stencil(jnp.pad(field, ((0, 0), (1, 1), (1, 1), (0, 0))))


def segment_rows(flat, seg_ids, count):
    return jax.vmap(lambda row: jax.ops.segment_sum(row, seg_ids, num_segments=count))(flat)


def reference(right_side, fine_ids, coarse_diag, coarse_links, coarse_ids, coarsest_inverse):
    id_tiles = fine_ids.reshape(N_GX, CX, N_GY, CY, CZ).transpose(0, 2, 1, 3, 4).reshape(N_GX, N_GY, -1)

    def to_tiles(field):
        return field.reshape(RHS, N_GX, CX, N_GY, CY, CZ).transpose(0, 1, 3, 2, 4, 5).reshape(RHS, N_GX, N_GY, -1)

    def from_tiles(tiles):
        return tiles.reshape(RHS, N_GX, N_GY, CX, CY, CZ).transpose(0, 1, 3, 2, 4, 5).reshape(RHS, N_GX * CX, N_GY * CY, CZ)

    def to_coarse(tiles):
        return tiles.reshape(RHS, N_GX, N_GY, AX, AY, AZ).transpose(0, 1, 3, 2, 4, 5).reshape(RHS, NAX, NAY, AZ)

    def from_coarse(grid):
        return grid.reshape(RHS, N_GX, AX, N_GY, AY, AZ).transpose(0, 1, 3, 2, 4, 5).reshape(RHS, N_GX, N_GY, CAGG)

    def seg_one(data, seg_ids):
        return jax.ops.segment_sum(data, seg_ids, num_segments=CAGG)

    restrict = jax.vmap(jax.vmap(jax.vmap(seg_one)), in_axes=(0, None))

    def coarse_apply(vector):
        padded = jnp.pad(vector, ((0, 0), (1, 1), (1, 1), (0, 0)))
        along = jnp.pad(vector, ((0, 0), (0, 0), (0, 0), (1, 1)))
        linked = coarse_links[0] * padded[:, :-2, 1:-1, :] + coarse_links[1] * padded[:, 2:, 1:-1, :]
        linked = linked + coarse_links[2] * padded[:, 1:-1, :-2, :] + coarse_links[3] * padded[:, 1:-1, 2:, :]
        linked = linked + coarse_links[4] * along[:, :, :, :-2] + coarse_links[5] * along[:, :, :, 2:]
        return coarse_diag * vector - linked

    coarse_inv_diag = 1.0 / coarse_diag
    pre_fine = chebyshev(fine_apply, 1.0 / 6.0, right_side, None, fine_low, fine_high)
    fine_residual = right_side - fine_apply(pre_fine)
    smoothed = fine_residual - prolong_weight * fine_apply(fine_residual)
    coarse_target = to_coarse(restrict(to_tiles(smoothed), id_tiles))
    pre_coarse = chebyshev(coarse_apply, coarse_inv_diag, coarse_target, None, coarse_low, coarse_high)
    coarse_residual = coarse_target - coarse_apply(pre_coarse)
    flat_ids = coarse_ids.reshape(-1)
    coarsest_target = segment_rows(coarse_residual.reshape(RHS, -1), flat_ids, NC2)
    coarsest = jnp.dot(coarsest_target, coarsest_inverse.T, precision=lax.Precision.HIGHEST)
    start = pre_coarse + coarsest[:, flat_ids].reshape(pre_coarse.shape)
    post_coarse = chebyshev(coarse_apply, coarse_inv_diag, coarse_target, start, coarse_low, coarse_high)
    post_tiles = from_coarse(post_coarse)
    index_full = jnp.broadcast_to(id_tiles[None], (RHS,) + id_tiles.shape)
    lifted = from_tiles(jnp.take_along_axis(post_tiles, index_full, axis=3))
    corrected = pre_fine + (lifted - prolong_weight * fine_apply(lifted))
    return chebyshev(fine_apply, 1.0 / 6.0, right_side, corrected, fine_low, fine_high)
```

```python
import math

import jax
import jax.numpy as jnp
import numpy as np
from jax import lax
from jax.experimental import pallas as pl
from jax.experimental.pallas import tpu as pltpu
from jax.sharding import PartitionSpec as P

F32 = jnp.float32
BF16 = jnp.bfloat16

PROLONG = 1.0 / 9.0


def nodes(low, high):
    theta = (high + low) / 2.0
    delta = (high - low) / 2.0
    reach = delta * math.cos(math.pi / 6.0)
    return (theta + reach, theta - reach, theta)


FINE_NODES = tuple(6.0 * node for node in nodes(2.0 / 30.0, 2.0))
COARSE_NODES = nodes(0.19, 1.9)

RHS, CX, YT, CY, CZ = 8, 4, 8, 8, 256
GX, GY = 16, 8
LANES = 128
NC2 = 2048
HI = NC2 // LANES


def beside_in_row(row):
    sub = lax.broadcasted_iota(jnp.int32, row.shape, 1)
    lane = lax.broadcasted_iota(jnp.int32, row.shape, 2)
    zero_tile = jnp.zeros((1,) + row.shape[1:], F32)
    up = pltpu.roll(row, 1, 1)
    up = jnp.where(sub == 0, jnp.concatenate([zero_tile, up[:-1]], axis=0), up)
    down = pltpu.roll(row, CY - 1, 1)
    down = jnp.where(sub == CY - 1, jnp.concatenate([down[1:], zero_tile], axis=0), down)
    left = jnp.where(lane == 0, 0.0, pltpu.roll(row, 1, 2))
    right = jnp.where(lane == CZ - 1, 0.0, pltpu.roll(row, CZ - 1, 2))
    return (up + down) + (left + right)


def relax(low, row, high, node):
    return (1.0 - 6.0 / node) * row + (1.0 / node) * (low + high + beside_in_row(row))


def row_gate(x, keep_low, keep_high):
    return jnp.where(x < 0, keep_low, jnp.where(x >= CX, keep_high, 1.0))


def beside_grid(grid):
    sub = lax.broadcasted_iota(jnp.int32, grid.shape, 1)
    lane = lax.broadcasted_iota(jnp.int32, grid.shape, 2)
    turned = pltpu.roll(grid, LANES // 2, 2)
    low_y = jnp.where(lane < LANES // 2, pltpu.roll(turned, 1, 1), turned)
    high_y = jnp.where(lane < LANES // 2, turned, pltpu.roll(turned, YT - 1, 1))
    low_z = pltpu.roll(grid, 1, 2)
    high_z = pltpu.roll(grid, LANES - 1, 2)
    del sub
    return low_y, high_y, low_z, high_z


def lower_of(grid):
    return jnp.concatenate([jnp.zeros((1,) + grid.shape[1:], F32), grid[:-1]], axis=0)


def upper_of(grid):
    return jnp.concatenate([grid[1:], jnp.zeros((1,) + grid.shape[1:], F32)], axis=0)


def load_window(coefs_ref, place, rows, before):
    diag, ux, uy, uz, ids = [], [], [], [], []
    for w in range(rows):
        dev = place + (w - before) // 2
        half = (w - before) % 2
        inside = jnp.logical_and(dev >= 0, dev < GX)
        at = jnp.clip(dev, 0, GX - 1)
        diag.append(jnp.where(inside, coefs_ref[at, 0, half], 1.0))
        ux.append(jnp.where(inside, coefs_ref[at, 1, half], 0.0))
        uy.append(jnp.where(inside, coefs_ref[at, 2, half], 0.0))
        uz.append(jnp.where(inside, coefs_ref[at, 3, half], 0.0))
        ids.append(coefs_ref[at, 4, half].astype(jnp.int32))
    diag, ux, uy, uz, ids = (jnp.stack(v, axis=0) for v in (diag, ux, uy, uz, ids))
    low_x = lower_of(ux)
    low_y = beside_grid(uy)[0]
    low_z = beside_grid(uz)[2]
    return (diag, low_x, ux, low_y, uy, low_z, uz), ids


def coarse_apply(grid, coefs):
    diag, lx, ux, ly, uy, lz, uz = coefs
    low_y, high_y, low_z, high_z = beside_grid(grid)
    linked = lx * lower_of(grid) + ux * upper_of(grid)
    linked = linked + ly * low_y + uy * high_y
    linked = linked + lz * low_z + uz * high_z
    return diag * grid - linked


def coarse_smooth(residual, coefs, inverse, with_last):
    total = None
    for k, node in enumerate(COARSE_NODES):
        update = (1.0 / node) * inverse * residual
        total = update if total is None else total + update
        if k < 2 or with_last:
            residual = residual - coarse_apply(update, coefs)
    return total, residual


def split3(value):
    first = value.astype(BF16)
    rest = value - first.astype(F32)
    second = rest.astype(BF16)
    third = (rest - second.astype(F32)).astype(BF16)
    return first, second, third


def down_kernel(place_ref, tl_ref, to_ref, tr_ref, ids_ref, coefs_ref, pool_ref, send_ref, u_ref, a_ref, b_ref):
    place = place_ref[0]
    keep_low = jnp.where(place > 0, 1.0, 0.0).astype(F32)
    keep_high = jnp.where(place < GX - 1, 1.0, 0.0).astype(F32)
    first, second, third = FINE_NODES
    for x in range(CX):
        a_ref[x] = tl_ref[:, x]
        a_ref[CX + x] = to_ref[:, x]
        a_ref[2 * CX + x] = tr_ref[:, x]

    def step(src, dst, reach, node):
        def body(k, carry):
            row = relax(src[k - 1], src[k], src[k + 1], node)
            dst[k] = row * row_gate(k - CX, keep_low, keep_high)
            return carry

        lax.fori_loop(CX - reach, 2 * CX + reach, body, 0)

    step(a_ref, b_ref, 3, first)

    def start_u(k, carry):
        u_ref[k] = (1.0 / first) * a_ref[k + 2] + (1.0 / second) * b_ref[k + 2]
        return carry

    lax.fori_loop(0, 8, start_u, 0)
    step(b_ref, a_ref, 2, second)

    def end_u(k, carry):
        u_ref[k] = u_ref[k] + (1.0 / third) * a_ref[k + 2]
        return carry

    lax.fori_loop(0, 8, end_u, 0)
    step(a_ref, b_ref, 1, third)
    step(b_ref, a_ref, 0, 1.0 / PROLONG)

    shape = (YT, CY, CZ)
    home = lax.broadcasted_iota(jnp.int32, shape, 2) // 4
    codes = []
    for x in range(CX):
        ids = ids_ref[:, x]
        codes.append((ids >> 6) * 3 + ((ids & 63) - home) + 1)
    pooled = []
    for half in range(2):
        parts = []
        for k in range(6):
            total = jnp.zeros(shape, F32)
            for x in range(CX):
                total = total + jnp.where(codes[x] == half * 6 + k, a_ref[CX + x], 0.0)
            parts.append(jnp.sum(total, axis=1))
        pooled.append(jnp.concatenate(parts, axis=1))
    pooled = jnp.concatenate(pooled, axis=0)
    pieces = jnp.concatenate(split3(pooled), axis=0)
    sums = jnp.dot(pieces, pool_ref[...], preferred_element_type=F32)
    rows = 2 * YT
    target = sums[:rows] + sums[rows : 2 * rows] + sums[2 * rows :]
    own = (target[:YT], target[YT:])

    coefs, ids = load_window(coefs_ref, place, 8, 3)
    blank = jnp.zeros((YT, LANES), F32)
    grid = jnp.stack([blank] * 3 + list(own) + [blank] * 3, axis=0)
    unused, residual = coarse_smooth(grid, coefs, 1.0 / coefs[0], True)
    high_of = ids >> 7
    low_of = ids & (LANES - 1)
    high_iota = lax.broadcasted_iota(jnp.int32, (HI, LANES), 0)
    low_iota = lax.broadcasted_iota(jnp.int32, (LANES, LANES), 0)
    counted = jnp.zeros((3 * HI, LANES), F32)
    for w in range(8):
        left, right = [], []
        for k in range(YT):
            picked = jnp.where(high_of[w, k : k + 1] == high_iota, residual[w, k : k + 1], 0.0)
            left.append(jnp.concatenate(split3(picked), axis=0))
            right.append(jnp.where(low_of[w, k : k + 1] == low_iota, 1.0, 0.0).astype(BF16))
        counted = counted + lax.dot_general(
            jnp.concatenate(left, axis=1),
            jnp.concatenate(right, axis=1),
            (((1,), (1,)), ((), ())),
            preferred_element_type=F32,
        )
    counted = counted[:HI] + counted[HI : 2 * HI] + counted[2 * HI :]
    for k in range(GX):
        send_ref[k, 0] = own[0]
        send_ref[k, 1] = own[1]
        send_ref[k, 2] = counted[:8]
        send_ref[k, 3] = counted[8:]


def solve_kernel(got_ref, inverse_ref, send_ref):
    top = got_ref[0, 2]
    bottom = got_ref[0, 3]
    for k in range(1, GX):
        top = top + got_ref[k, 2]
        bottom = bottom + got_ref[k, 3]
    target = jnp.concatenate([top, bottom], axis=0)
    total = jnp.zeros((LANES, LANES), F32)
    for k in range(HI):
        total = total + inverse_ref[:, k * LANES : (k + 1) * LANES] * target[k : k + 1]
    row = jnp.sum(total.T, axis=0, keepdims=True)
    tile = jnp.broadcast_to(row, (8, LANES))
    for k in range(GX):
        send_ref[k] = tile


def lane_take(table, index):
    return jnp.take_along_axis(table, index, axis=1, mode="promise_in_bounds")


def up_kernel(
    place_ref,
    got_ref,
    table_ref,
    coefs_ref,
    idl_ref,
    ido_ref,
    idr_ref,
    u_ref,
    ul_ref,
    ur_ref,
    out_ref,
    post_ref,
    a_ref,
    b_ref,
):
    place = place_ref[0]
    keep_low = jnp.where(place > 0, 1.0, 0.0).astype(F32)
    keep_high = jnp.where(place < GX - 1, 1.0, 0.0).astype(F32)
    rows, before = 16, 7
    coefs, ids = load_window(coefs_ref, place, rows, before)
    target = []
    for w in range(rows):
        dev = place + (w - before) // 2
        inside = jnp.logical_and(dev >= 0, dev < GX)
        at = jnp.clip(dev, 0, GX - 1)
        target.append(jnp.where(inside, got_ref[at, (w - before) % 2], 0.0))
    target = jnp.stack(target, axis=0)
    inverse = 1.0 / coefs[0]
    pre, left_over = coarse_smooth(target, coefs, inverse, True)
    high_of = ids >> 7
    low_of = ids & (LANES - 1)
    lifted_rows = []
    for w in range(rows):
        value = jnp.zeros((YT, LANES), F32)
        for k in range(HI):
            table = jnp.broadcast_to(table_ref[k, 0:1], (YT, LANES))
            value = jnp.where(high_of[w] == k, lane_take(table, low_of[w]), value)
        lifted_rows.append(value)
    coarsest = jnp.stack(lifted_rows, axis=0)
    left_over = left_over - coarse_apply(coarsest, coefs)
    update, unused = coarse_smooth(left_over, coefs, inverse, False)
    post = pre + coarsest + update
    for k in range(6):
        gate = keep_low if k < 2 else (keep_high if k >= 4 else None)
        row = post[k + 5]
        post_ref[k] = row if gate is None else row * gate

    for slab, id_ref in enumerate((idl_ref, ido_ref, idr_ref)):

        def lift(x, carry, slab=slab, id_ref=id_ref):
            for k in range(YT):
                table0 = jnp.broadcast_to(post_ref[2 * slab, k : k + 1], (CY, LANES))
                table1 = jnp.broadcast_to(post_ref[2 * slab + 1, k : k + 1], (CY, LANES))
                for part in range(2):
                    lanes = slice(part * LANES, (part + 1) * LANES)
                    cell = id_ref[k, x, :, lanes]
                    low = cell & (LANES - 1)
                    value = jnp.where(cell >= LANES, lane_take(table1, low), lane_take(table0, low))
                    a_ref[slab * CX + x, k, :, lanes] = value
            return carry

        lax.fori_loop(0, CX, lift, 0)

    def step(src, dst, reach, node, add):
        def body(k, carry):
            row = relax(src[k - 1], src[k], src[k + 1], node)
            row = row * row_gate(k - CX, keep_low, keep_high)
            if add:
                row = row + u_ref[k - 2]
            dst[k] = row
            return carry

        lax.fori_loop(CX - reach, 2 * CX + reach, body, 0)

    step(a_ref, b_ref, 2, 1.0 / PROLONG, True)
    for at, edge, gate in ((1, ul_ref, keep_low), (2 * CX + 2, ur_ref, keep_high)):
        row = relax(a_ref[at - 1], a_ref[at], a_ref[at + 1], 1.0 / PROLONG)
        b_ref[at] = row * gate + edge[...]
    first, second, third = FINE_NODES
    step(b_ref, a_ref, 2, first, False)
    step(a_ref, b_ref, 1, second, False)
    for x in range(CX):
        k = CX + x
        out_ref[:, x] = relax(b_ref[k - 1], b_ref[k], b_ref[k + 1], third) + u_ref[k - 2]


def pool_matrix():
    cell = np.arange(CZ)
    out = np.zeros((2, 3, CZ, LANES), np.float32)
    for half in range(2):
        for shift in range(3):
            at = cell // 4 + shift - 1
            ok = (at >= 0) & (at < 64)
            out[half, shift, cell[ok], half * 64 + at[ok]] = 1.0
    return out.reshape(6 * CZ, LANES)


def call(kernel, out_shape, scratch, flops, scalars=0):
    def spec(k):
        return pl.BlockSpec(memory_space=pltpu.SMEM if k < scalars else pltpu.VMEM)

    def run(*args):
        return pl.pallas_call(
            kernel,
            out_shape=out_shape,
            in_specs=[spec(k) for k in range(len(args))],
            out_specs=jax.tree.map(lambda _: pl.BlockSpec(memory_space=pltpu.VMEM), out_shape),
            scratch_shapes=scratch,
            compiler_params=pltpu.CompilerParams(vmem_limit_bytes=40 * 1024 * 1024),
            cost_estimate=pl.CostEstimate(flops=flops, bytes_accessed=2**20, transcendentals=0),
        )(*args)

    return run


def shape_of(*dims):
    return jax.ShapeDtypeStruct(dims, F32)


def to_all(value, axis, count):
    return lax.all_to_all(jnp.broadcast_to(value[None], (count,) + value.shape), axis, 0, 0, tiled=True)


def beside(value_up, value_down):
    forward = [(k, k + 1) for k in range(GX - 1)]
    backward = [(b, a) for a, b in forward]
    return lax.ppermute(value_up, "gx", forward), lax.ppermute(value_down, "gx", backward)


def local(right_side, fine_ids, coarse_diag, coarse_links, coarse_ids, coarsest_inverse):
    place = lax.axis_index("gx").astype(jnp.int32).reshape(1)
    own = lax.all_to_all(right_side, "gy", 0, 0, tiled=True)
    low, high = beside(own, own)

    coefs = jnp.stack(
        [coarse_diag, coarse_links[1], coarse_links[3], coarse_links[5], coarse_ids.astype(F32)], axis=0
    ).reshape(5, 2, LANES)
    coefs = to_all(coefs, "gy", GY).transpose(1, 2, 0, 3)
    coefs = to_all(coefs, "gx", GX)
    ids = to_all(fine_ids, "gy", GY)
    id_low, id_high = beside(ids, ids)
    inverse = to_all(coarsest_inverse, "gy", GY).reshape(LANES, NC2)

    pool = jnp.asarray(pool_matrix(), BF16)
    field = (3 * CX, YT, CY, CZ)
    send, u = call(
        down_kernel,
        [shape_of(GX, 4, YT, LANES), shape_of(8, YT, CY, CZ)],
        [pltpu.VMEM(field, F32), pltpu.VMEM(field, F32)],
        10**7,
        1,
    )(place, low, own, high, ids, coefs, pool)
    got = lax.all_to_all(send, "gx", 0, 0, tiled=True)
    u_low, u_high = beside(u[3], u[4])
    send = call(solve_kernel, shape_of(GX, 8, LANES), [], 10**6)(got, inverse)
    table = lax.all_to_all(send, "gx", 0, 0, tiled=True)
    out = call(
        up_kernel,
        shape_of(YT, CX, CY, CZ),
        [pltpu.VMEM((6, YT, LANES), F32), pltpu.VMEM(field, F32), pltpu.VMEM(field, F32)],
        10**7,
        1,
    )(place, got, table, coefs, id_low, ids, id_high, u, u_low, u_high)
    return lax.all_to_all(out, "gy", 0, 0, tiled=True)


def solution(mesh):
    return jax.shard_map(
        local,
        mesh=mesh,
        in_specs=(
            P(None, "gx", "gy", None),
            P("gx", "gy", None),
            P("gx", "gy", None),
            P(None, "gx", "gy", None),
            P("gx", "gy", None),
            P(("gx", "gy"), None),
        ),
        out_specs=P(None, "gx", "gy", None),
        check_vma=False,
    )
```

```python
import math

import jax
import jax.numpy as jnp
from jax import lax
from jax.experimental import pallas as pl
from jax.experimental.pallas import tpu as pltpu
from jax.sharding import PartitionSpec as P

F32 = jnp.float32
BF16 = jnp.bfloat16

PROLONG = 1.0 / 9.0


def nodes(low, high):
    theta = (high + low) / 2.0
    delta = (high - low) / 2.0
    reach = delta * math.cos(math.pi / 6.0)
    return (theta + reach, theta - reach, theta)


FINE_NODES = tuple(6.0 * node for node in nodes(2.0 / 30.0, 2.0))
COARSE_NODES = nodes(0.19, 1.9)

RHS, CX, YT, CY, CZ = 8, 4, 8, 8, 256
GX, GY = 16, 8
LANES = 128
NC2 = 2048
HI = NC2 // LANES


def beside_in_row(row):
    sub = lax.broadcasted_iota(jnp.int32, row.shape, 1)
    lane = lax.broadcasted_iota(jnp.int32, row.shape, 2)
    zero_tile = jnp.zeros((1,) + row.shape[1:], F32)
    up = pltpu.roll(row, 1, 1)
    up = jnp.where(sub == 0, jnp.concatenate([zero_tile, up[:-1]], axis=0), up)
    down = pltpu.roll(row, CY - 1, 1)
    down = jnp.where(sub == CY - 1, jnp.concatenate([down[1:], zero_tile], axis=0), down)
    left = jnp.where(lane == 0, 0.0, pltpu.roll(row, 1, 2))
    right = jnp.where(lane == CZ - 1, 0.0, pltpu.roll(row, CZ - 1, 2))
    return (up + down) + (left + right)


def relax(low, row, high, node):
    return (1.0 - 6.0 / node) * row + (1.0 / node) * (low + high + beside_in_row(row))


def beside_grid(grid):
    sub = lax.broadcasted_iota(jnp.int32, grid.shape, 1)
    lane = lax.broadcasted_iota(jnp.int32, grid.shape, 2)
    turned = pltpu.roll(grid, LANES // 2, 2)
    low_y = jnp.where(lane < LANES // 2, pltpu.roll(turned, 1, 1), turned)
    high_y = jnp.where(lane < LANES // 2, turned, pltpu.roll(turned, YT - 1, 1))
    low_z = pltpu.roll(grid, 1, 2)
    high_z = pltpu.roll(grid, LANES - 1, 2)
    del sub
    return low_y, high_y, low_z, high_z


def lower_of(grid):
    return jnp.concatenate([jnp.zeros((1,) + grid.shape[1:], F32), grid[:-1]], axis=0)


def upper_of(grid):
    return jnp.concatenate([grid[1:], jnp.zeros((1,) + grid.shape[1:], F32)], axis=0)


NAX = 2 * GX
WINDOW = 10
FIELDS = 5


def with_lower(diag, ux, uy, uz):
    return (diag, lower_of(ux), ux, beside_grid(uy)[0], uy, beside_grid(uz)[2], uz, 1.0 / diag)


def coarse_apply(grid, coefs, below=None, above=None):
    diag, lx, ux, ly, uy, lz, uz = coefs[:7]
    low_y, high_y, low_z, high_z = beside_grid(grid)
    low_x = lower_of(grid) if below is None else jnp.concatenate([below[None], grid[:-1]], axis=0)
    high_x = upper_of(grid) if above is None else jnp.concatenate([grid[1:], above[None]], axis=0)
    linked = lx * low_x + ux * high_x
    linked = linked + ly * low_y + uy * high_y
    linked = linked + lz * low_z + uz * high_z
    return diag * grid - linked


def coarse_smooth(residual, coefs, with_last):
    total = None
    for k, node in enumerate(COARSE_NODES):
        update = (1.0 / node) * coefs[7] * residual
        total = update if total is None else total + update
        if k < 2 or with_last:
            residual = residual - coarse_apply(update, coefs)
    return total, residual


def split3(value):
    first = value.astype(BF16)
    rest = value - first.astype(F32)
    second = rest.astype(BF16)
    third = (rest - second.astype(F32)).astype(BF16)
    return first, second, third


def tiles_kernel(ids_ref, diag_ref, links_ref, coarse_ids_ref, out_ref, id_buf, diag_buf, link_buf, cid_buf, sems):
    pairs = ((ids_ref, id_buf), (diag_ref, diag_buf), (links_ref, link_buf), (coarse_ids_ref, cid_buf))
    copies = [pltpu.make_async_copy(src, dst, sems.at[k]) for k, (src, dst) in enumerate(pairs)]
    for copy in copies:
        copy.start()
    for copy in copies:
        copy.wait()
    fields = (
        diag_buf[...],
        link_buf[1],
        link_buf[3],
        link_buf[5],
        cid_buf[...].astype(F32),
    )
    rows = [
        jnp.concatenate([field[half, k : k + 1] for half in range(2) for k in range(2)], axis=1)
        for field in fields
    ]
    rows.append(jnp.zeros((3, CZ), F32))
    for x in range(CX):
        out_ref[x] = id_buf[x].astype(F32)
    out_ref[CX] = jnp.concatenate(rows, axis=0)


SHARED = 3 * CX + 1


def share_kernel(mine_ref, low_ref, high_ref, out_ref):
    out_ref[0 : CX + 1] = mine_ref[...]
    out_ref[CX + 1 : 2 * CX + 1] = low_ref[...]
    out_ref[2 * CX + 1 :] = high_ref[...]


def shared_tile(near_ref, far_ref, chip, core, j, tile):
    k = lax.rem(chip + 4 - j // 2, 4)
    return jnp.where(core == j % 2, near_ref[k, tile], far_ref[k, tile])


def shared_ids(near_ref, far_ref, chip, core, tile):
    rows = [shared_tile(near_ref, far_ref, chip, core, j, tile) for j in range(GY)]
    return jnp.stack(rows, axis=0).astype(jnp.int32)


def pool_matrix():
    lane = lax.broadcasted_iota(jnp.int32, (CZ, LANES), 1)
    gap = lane - lax.broadcasted_iota(jnp.int32, (CZ, LANES), 0) // 4
    parts = []
    for half in range(2):
        for shift in range(-1, 2):
            hit = jnp.logical_and(gap == half * 64 + shift, lane // 64 == half)
            parts.append(jnp.where(hit, 1.0, 0.0).astype(BF16))
    return jnp.concatenate(parts, axis=0)


EDGE = 4
ROWS = CX + 2 * EDGE
U_EDGE = 2


def relax_rows(src, dst, reach, node, keep_low, keep_high, plus=None):
    for k in range(EDGE - reach, EDGE + CX + reach):
        row = relax(src[k - 1], src[k], src[k + 1], node)
        if k < EDGE:
            row = row * keep_low
        elif k >= EDGE + CX:
            row = row * keep_high
        dst[k] = row if plus is None else row + plus[k - EDGE + U_EDGE]


def down_kernel(where_ref, tl_ref, to_ref, tr_ref, smooth_ref, u_ref, up_ref, down_ref, a_ref, b_ref):
    place = where_ref[0]
    keep_low = jnp.where(place > 0, 1.0, 0.0).astype(F32)
    keep_high = jnp.where(place < GX - 1, 1.0, 0.0).astype(F32)
    gates = keep_low, keep_high
    first, second, third = FINE_NODES
    for x in range(CX):
        a_ref[x] = tl_ref[:, x] * keep_low
        a_ref[EDGE + x] = to_ref[:, x]
        a_ref[EDGE + CX + x] = tr_ref[:, x] * keep_high

    relax_rows(a_ref, b_ref, 3, first, *gates)
    shift = EDGE - U_EDGE
    for k in range(CX + 2 * U_EDGE):
        u_ref[k] = (1.0 / first) * a_ref[k + shift] + (1.0 / second) * b_ref[k + shift]
    relax_rows(b_ref, a_ref, 2, second, *gates)
    for k in range(CX + 2 * U_EDGE):
        u_ref[k] = u_ref[k] + (1.0 / third) * a_ref[k + shift]
    up_ref[...] = u_ref[U_EDGE + 1]
    down_ref[...] = u_ref[U_EDGE + 2]
    relax_rows(a_ref, b_ref, 1, third, *gates)
    for x in range(CX):
        k = EDGE + x
        smooth_ref[x] = relax(b_ref[k - 1], b_ref[k], b_ref[k + 1], 1.0 / PROLONG)


def pool_kernel(where_ref, smooth_ref, near_ref, far_ref, send_ref, tile_ref):
    chip, core = where_ref[1], where_ref[2]
    shape = (YT, CY, CZ)
    home = lax.broadcasted_iota(jnp.int32, shape, 2) // 4
    codes = []
    for x in range(CX):
        ids = shared_ids(near_ref, far_ref, chip, core, x)
        codes.append((ids >> 6) * 3 + ((ids & 63) - home) + 1)
    pooled = []
    for half in range(2):
        parts = []
        for k in range(6):
            total = jnp.zeros(shape, F32)
            for x in range(CX):
                total = total + jnp.where(codes[x] == half * 6 + k, smooth_ref[x], 0.0)
            parts.append(jnp.sum(total, axis=1))
        pooled.append(jnp.concatenate(parts, axis=1))
    pooled = jnp.concatenate(pooled, axis=0)
    pieces = jnp.concatenate(split3(pooled), axis=0)
    sums = jnp.dot(pieces, pool_matrix(), preferred_element_type=F32)
    rows = 2 * YT
    target = sums[:rows] + sums[rows : 2 * rows] + sums[2 * rows :]
    tiles = [target[:YT], target[YT:]]
    for j in range(GY):
        tile_ref[j] = shared_tile(near_ref, far_ref, chip, core, j, CX)
    for k in range(FIELDS):
        for half in range(2):
            tiles.append(tile_ref[:, k, half * LANES : (half + 1) * LANES])
    for i in range(GX):
        for k, tile in enumerate(tiles):
            send_ref[i, k] = tile


def solve_kernel(where_ref, got_ref, near_ref, far_ref, send_ref, window_ref, full_ref, total_ref):
    def grid(k):
        return jnp.stack([got_ref[x // 2, 2 * k + x % 2] for x in range(NAX)], axis=0)

    coefs = with_lower(grid(1), grid(2), grid(3), grid(4))
    pre, residual = coarse_smooth(grid(0), coefs, True)
    for k, value in enumerate((*coefs, pre, residual)):
        full_ref[k] = value
    place = where_ref[0]
    for k in range(10):
        for w in range(WINDOW):
            x = 2 * place + w - 4
            row = full_ref[k, jnp.clip(x, 0, NAX - 1)]
            if not 4 <= w < 6:
                row = jnp.where(jnp.logical_and(x >= 0, x < NAX), row, 1.0 if k in (0, 7) else 0.0)
            window_ref[k, w] = row
    ids = grid(5).astype(jnp.int32)
    high_of = ids >> 7
    low_of = ids & (LANES - 1)
    high_iota = lax.broadcasted_iota(jnp.int32, (HI, LANES), 0)
    low_iota = lax.broadcasted_iota(jnp.int32, (LANES, LANES), 0)
    counted = jnp.zeros((3 * HI, LANES), F32)
    for x in range(NAX):
        left, right = [], []
        for k in range(YT):
            picked = jnp.where(high_of[x, k : k + 1] == high_iota, residual[x, k : k + 1], 0.0)
            left.append(jnp.concatenate(split3(picked), axis=0))
            right.append(jnp.where(low_of[x, k : k + 1] == low_iota, 1.0, 0.0).astype(BF16))
        counted = counted + lax.dot_general(
            jnp.concatenate(left, axis=1),
            jnp.concatenate(right, axis=1),
            (((1,), (1,)), ((), ())),
            preferred_element_type=F32,
        )
    target = counted[:HI] + counted[HI : 2 * HI] + counted[2 * HI :]
    chip, core = where_ref[1], where_ref[2]
    for ref, side in ((near_ref, core), (far_ref, 1 - core)):
        for k in range(4):
            total = jnp.zeros((HI, LANES), F32)
            for h in range(HI):
                total = total + ref[k, :, h * LANES : (h + 1) * LANES] * target[h : h + 1]
            at = lax.rem(chip + 4 - k, 4) * 2 + side
            total_ref[pl.ds(pl.multiple_of(at * HI, HI), HI)] = total
    row = jnp.sum(total_ref[...].T, axis=0, keepdims=True)
    tile = jnp.broadcast_to(row, (8, LANES))
    for i in range(GX):
        send_ref[i] = tile


def lane_take(table, index):
    return jnp.take_along_axis(table, index, axis=1, mode="promise_in_bounds")


def up_kernel(
    where_ref,
    table_ref,
    window_ref,
    got_ref,
    near_ref,
    far_ref,
    u_ref,
    ul_ref,
    ur_ref,
    out_ref,
    post_ref,
    a_ref,
    b_ref,
):
    place, chip, core = where_ref[0], where_ref[1], where_ref[2]
    keep_low = jnp.where(place > 0, 1.0, 0.0).astype(F32)
    keep_high = jnp.where(place < GX - 1, 1.0, 0.0).astype(F32)
    coefs = tuple(window_ref[k] for k in range(8))
    picked = []
    for w in range(-5, 7):
        unknown = got_ref[jnp.clip(place + w // 2, 0, GX - 1), 2 * FIELDS + w % 2].astype(jnp.int32)
        high_of = unknown >> 7
        low_of = unknown & (LANES - 1)
        value = jnp.zeros((YT, LANES), F32)
        for k in range(HI):
            table = jnp.broadcast_to(table_ref[k, 0:1], (YT, LANES))
            value = jnp.where(high_of == k, lane_take(table, low_of), value)
        picked.append(value)
    coarsest = jnp.stack(picked[1:-1], axis=0)
    rest = window_ref[9] - coarse_apply(coarsest, coefs, picked[0], picked[-1])
    update, unused = coarse_smooth(rest, coefs, False)
    post = window_ref[8] + coarsest + update
    for k in range(6):
        gate = keep_low if k < 2 else (keep_high if k >= 4 else None)
        row = post[k + 2]
        post_ref[k] = row if gate is None else row * gate

    for slab, first_tile in ((0, CX + 1), (1, 0), (2, 2 * CX + 1)):
        for x in range(CX):
            ids = shared_ids(near_ref, far_ref, chip, core, first_tile + x)
            for k in range(YT):
                table0 = jnp.broadcast_to(post_ref[2 * slab, k : k + 1], (CY, LANES))
                table1 = jnp.broadcast_to(post_ref[2 * slab + 1, k : k + 1], (CY, LANES))
                for part in range(2):
                    lanes = slice(part * LANES, (part + 1) * LANES)
                    cell = ids[k, :, lanes]
                    low = cell & (LANES - 1)
                    value = jnp.where(cell >= LANES, lane_take(table1, low), lane_take(table0, low))
                    a_ref[slab * CX + x, k, :, lanes] = value

    gates = keep_low, keep_high
    first, second, third = FINE_NODES
    relax_rows(a_ref, b_ref, 2, 1.0 / PROLONG, *gates, plus=u_ref)
    for k, u, gate in ((EDGE - 3, ul_ref, keep_low), (EDGE + CX + 2, ur_ref, keep_high)):
        b_ref[k] = (relax(a_ref[k - 1], a_ref[k], a_ref[k + 1], 1.0 / PROLONG) + u[...]) * gate
    relax_rows(b_ref, a_ref, 2, first, *gates)
    relax_rows(a_ref, b_ref, 1, second, *gates)
    for x in range(CX):
        k = EDGE + x
        out_ref[:, x] = relax(b_ref[k - 1], b_ref[k], b_ref[k + 1], third) + u_ref[U_EDGE + x]


def call(kernel, out_shape, scratch, flops, scalars=0, inputs=pltpu.VMEM, limit=24):
    def spec(k):
        return pl.BlockSpec(memory_space=pltpu.SMEM if k < scalars else inputs)

    def run(*args):
        return pl.pallas_call(
            kernel,
            out_shape=out_shape,
            in_specs=[spec(k) for k in range(len(args))],
            out_specs=jax.tree.map(lambda _: pl.BlockSpec(memory_space=pltpu.VMEM), out_shape),
            scratch_shapes=scratch,
            compiler_params=pltpu.CompilerParams(vmem_limit_bytes=limit * 1024 * 1024),
            cost_estimate=pl.CostEstimate(flops=flops, bytes_accessed=2**20, transcendentals=0),
        )(*args)

    return run


def shape_of(*dims):
    return jax.ShapeDtypeStruct(dims, F32)


def shifted(value, step):
    return lax.ppermute(value, "gx", [(k, (k + step) % GX) for k in range(GX)])


FINE_FLOPS = 3 * 10**10


def round_chips(value):
    return [lax.ppermute(value, "gy", [(j, (j + 2 * k) % GY) for j in range(GY)]) for k in range(1, 4)]


def other_core(value):
    return lax.ppermute(value, "gy", [(j, j ^ 1) for j in range(GY)])


def local(right_side, fine_ids, coarse_diag, coarse_links, coarse_ids, coarsest_inverse):
    row = lax.axis_index("gy")
    place = jnp.stack([lax.axis_index("gx"), row // 2, row % 2]).astype(jnp.int32)
    cells = lax.all_to_all(right_side, "gy", 0, 0, tiled=True)
    low, high = shifted(cells, 1), shifted(cells, -1)

    arguments = (fine_ids, coarse_diag, coarse_links, coarse_ids)
    tiles = call(
        tiles_kernel,
        pltpu.VMEM((CX + 1, CY, CZ), F32),
        [
            pltpu.VMEM((CX, CY, CZ), jnp.int32),
            pltpu.VMEM((2, 2, 64), F32),
            pltpu.VMEM((6, 2, 2, 64), F32),
            pltpu.VMEM((2, 2, 64), jnp.int32),
            pltpu.SemaphoreType.DMA((4,)),
        ],
        10**8,
        inputs=pltpu.HBM,
    )(*(pltpu.with_memory_space_constraint(value, pltpu.HBM) for value in arguments))
    shared = call(share_kernel, pltpu.VMEM((SHARED, CY, CZ), F32), [], 10**8)(
        tiles, shifted(tiles[:CX], 1), shifted(tiles[:CX], -1)
    )
    near = jnp.stack([shared, *round_chips(shared)], axis=0)
    far = other_core(near)

    field = (ROWS, YT, CY, CZ)
    smooth, u, going_up, going_down = call(
        down_kernel,
        [
            pltpu.VMEM((CX, YT, CY, CZ), F32),
            pltpu.VMEM((CX + 2 * U_EDGE, YT, CY, CZ), F32),
            pltpu.VMEM((YT, CY, CZ), F32),
            pltpu.VMEM((YT, CY, CZ), F32),
        ],
        [pltpu.VMEM(field, F32), pltpu.VMEM(field, F32)],
        FINE_FLOPS,
        1,
    )(place, low, cells, high)
    send = call(
        pool_kernel,
        pltpu.VMEM((GX, 2 + 2 * FIELDS, YT, LANES), F32),
        [pltpu.VMEM((GY, CY, CZ), F32)],
        2 * 10**9,
        1,
    )(place, smooth, near, far)
    send, inverse = lax.optimization_barrier((send, coarsest_inverse))
    inverse_near = jnp.stack([inverse, *round_chips(inverse)], axis=0)
    inverse_far = other_core(inverse_near)
    u_low, u_high = shifted(going_up, 1), shifted(going_down, -1)
    got = lax.all_to_all(send, "gx", 0, 0, tiled=True)
    send, window = call(
        solve_kernel,
        [pltpu.VMEM((GX, 8, LANES), F32), pltpu.VMEM((10, WINDOW, YT, LANES), F32)],
        [pltpu.VMEM((10, NAX, YT, LANES), F32), pltpu.VMEM((LANES, LANES), F32)],
        3 * 10**9,
        1,
    )(place, got, inverse_near, inverse_far)
    table = lax.all_to_all(send, "gx", 0, 0, tiled=True)
    out = call(
        up_kernel,
        pltpu.VMEM((YT, CX, CY, CZ), F32),
        [pltpu.VMEM((6, YT, LANES), F32), pltpu.VMEM(field, F32), pltpu.VMEM(field, F32)],
        4 * 10**9,
        1,
    )(place, table, window, got, near, far, u, u_low, u_high)
    return lax.all_to_all(out, "gy", 0, 0, tiled=True)


def solution(mesh):
    return jax.shard_map(
        local,
        mesh=mesh,
        in_specs=(
            P(None, "gx", "gy", None),
            P("gx", "gy", None),
            P("gx", "gy", None),
            P(None, "gx", "gy", None),
            P("gx", "gy", None),
            P(("gx", "gy"), None),
        ),
        out_specs=P(None, "gx", "gy", None),
        check_vma=False,
    )
```

```python
import math

import jax
import jax.numpy as jnp
from jax import lax
from jax.experimental import pallas as pl
from jax.experimental.pallas import tpu as pltpu
from jax.sharding import PartitionSpec as P

F32 = jnp.float32
BF16 = jnp.bfloat16

PROLONG = 1.0 / 9.0


def nodes(low, high):
    theta = (high + low) / 2.0
    delta = (high - low) / 2.0
    reach = delta * math.cos(math.pi / 6.0)
    return (theta + reach, theta - reach, theta)


FINE_NODES = tuple(6.0 * node for node in nodes(2.0 / 30.0, 2.0))
COARSE_NODES = nodes(0.19, 1.9)

RHS, CX, YT, CY, CZ = 8, 4, 8, 8, 256
GX, GY = 16, 8
LANES = 128
NC2 = 2048
HI = NC2 // LANES


def beside_in_row(row):
    sub = lax.broadcasted_iota(jnp.int32, row.shape, 1)
    lane = lax.broadcasted_iota(jnp.int32, row.shape, 2)
    zero_tile = jnp.zeros((1,) + row.shape[1:], F32)
    up = pltpu.roll(row, 1, 1)
    up = jnp.where(sub == 0, jnp.concatenate([zero_tile, up[:-1]], axis=0), up)
    down = pltpu.roll(row, CY - 1, 1)
    down = jnp.where(sub == CY - 1, jnp.concatenate([down[1:], zero_tile], axis=0), down)
    left = jnp.where(lane == 0, 0.0, pltpu.roll(row, 1, 2))
    right = jnp.where(lane == CZ - 1, 0.0, pltpu.roll(row, CZ - 1, 2))
    return (up + down) + (left + right)


def relax(low, row, high, node):
    return (1.0 - 6.0 / node) * row + (1.0 / node) * (low + high + beside_in_row(row))


def beside_grid(grid):
    sub = lax.broadcasted_iota(jnp.int32, grid.shape, 1)
    lane = lax.broadcasted_iota(jnp.int32, grid.shape, 2)
    turned = pltpu.roll(grid, LANES // 2, 2)
    low_y = jnp.where(lane < LANES // 2, pltpu.roll(turned, 1, 1), turned)
    high_y = jnp.where(lane < LANES // 2, turned, pltpu.roll(turned, YT - 1, 1))
    low_z = pltpu.roll(grid, 1, 2)
    high_z = pltpu.roll(grid, LANES - 1, 2)
    del sub
    return low_y, high_y, low_z, high_z


def lower_of(grid):
    return jnp.concatenate([jnp.zeros((1,) + grid.shape[1:], F32), grid[:-1]], axis=0)


def upper_of(grid):
    return jnp.concatenate([grid[1:], jnp.zeros((1,) + grid.shape[1:], F32)], axis=0)


NAX = 2 * GX
WINDOW = 10
FIELDS = 5


def with_lower(diag, ux, uy, uz):
    return (diag, lower_of(ux), ux, beside_grid(uy)[0], uy, beside_grid(uz)[2], uz, 1.0 / diag)


def coarse_apply(grid, coefs, below=None, above=None):
    diag, lx, ux, ly, uy, lz, uz = coefs[:7]
    low_y, high_y, low_z, high_z = beside_grid(grid)
    low_x = lower_of(grid) if below is None else jnp.concatenate([below[None], grid[:-1]], axis=0)
    high_x = upper_of(grid) if above is None else jnp.concatenate([grid[1:], above[None]], axis=0)
    linked = lx * low_x + ux * high_x
    linked = linked + ly * low_y + uy * high_y
    linked = linked + lz * low_z + uz * high_z
    return diag * grid - linked


def coarse_smooth(residual, coefs, with_last):
    total = None
    for k, node in enumerate(COARSE_NODES):
        update = (1.0 / node) * coefs[7] * residual
        total = update if total is None else total + update
        if k < 2 or with_last:
            residual = residual - coarse_apply(update, coefs)
    return total, residual


def split3(value):
    first = value.astype(BF16)
    rest = value - first.astype(F32)
    second = rest.astype(BF16)
    third = (rest - second.astype(F32)).astype(BF16)
    return first, second, third


def tiles_kernel(ids_ref, diag_ref, links_ref, coarse_ids_ref, out_ref, id_buf, diag_buf, link_buf, cid_buf, sems):
    pairs = ((ids_ref, id_buf), (diag_ref, diag_buf), (links_ref, link_buf), (coarse_ids_ref, cid_buf))
    copies = [pltpu.make_async_copy(src, dst, sems.at[k]) for k, (src, dst) in enumerate(pairs)]
    for copy in copies:
        copy.start()
    for copy in copies:
        copy.wait()
    fields = (
        diag_buf[...],
        link_buf[1],
        link_buf[3],
        link_buf[5],
        cid_buf[...].astype(F32),
    )
    rows = [
        jnp.concatenate([field[half, k : k + 1] for half in range(2) for k in range(2)], axis=1)
        for field in fields
    ]
    rows.append(jnp.zeros((3, CZ), F32))
    for x in range(CX):
        out_ref[x] = id_buf[x].astype(F32)
    out_ref[CX] = jnp.concatenate(rows, axis=0)


SHARED = 3 * CX + 1


def share_kernel(mine_ref, low_ref, high_ref, out_ref):
    out_ref[0 : CX + 1] = mine_ref[...]
    out_ref[CX + 1 : 2 * CX + 1] = low_ref[...]
    out_ref[2 * CX + 1 :] = high_ref[...]


def shared_tile(near_ref, far_ref, chip, core, j, tile):
    k = lax.rem(chip + 4 - j // 2, 4)
    return jnp.where(core == j % 2, near_ref[k, tile], far_ref[k, tile])


def shared_ids(near_ref, far_ref, chip, core, tile):
    rows = [shared_tile(near_ref, far_ref, chip, core, j, tile) for j in range(GY)]
    return jnp.stack(rows, axis=0).astype(jnp.int32)


def pool_matrix():
    lane = lax.broadcasted_iota(jnp.int32, (CZ, LANES), 1)
    gap = lane - lax.broadcasted_iota(jnp.int32, (CZ, LANES), 0) // 4
    parts = []
    for half in range(2):
        for shift in range(-1, 2):
            hit = jnp.logical_and(gap == half * 64 + shift, lane // 64 == half)
            parts.append(jnp.where(hit, 1.0, 0.0).astype(BF16))
    return jnp.concatenate(parts, axis=0)


EDGE = 4
ROWS = CX + 2 * EDGE
U_EDGE = 2


def relax_rows(src, dst, reach, node, keep_low, keep_high, plus=None):
    for k in range(EDGE - reach, EDGE + CX + reach):
        row = relax(src[k - 1], src[k], src[k + 1], node)
        if k < EDGE:
            row = row * keep_low
        elif k >= EDGE + CX:
            row = row * keep_high
        dst[k] = row if plus is None else row + plus[k - EDGE + U_EDGE]


def down_kernel(where_ref, tl_ref, to_ref, tr_ref, smooth_ref, u_ref, up_ref, down_ref, a_ref, b_ref):
    place = where_ref[0]
    keep_low = jnp.where(place > 0, 1.0, 0.0).astype(F32)
    keep_high = jnp.where(place < GX - 1, 1.0, 0.0).astype(F32)
    gates = keep_low, keep_high
    first, second, third = FINE_NODES
    for x in range(CX):
        a_ref[x] = tl_ref[:, x] * keep_low
        a_ref[EDGE + x] = to_ref[:, x]
        a_ref[EDGE + CX + x] = tr_ref[:, x] * keep_high

    relax_rows(a_ref, b_ref, 3, first, *gates)
    shift = EDGE - U_EDGE
    for k in range(CX + 2 * U_EDGE):
        u_ref[k] = (1.0 / first) * a_ref[k + shift] + (1.0 / second) * b_ref[k + shift]
    relax_rows(b_ref, a_ref, 2, second, *gates)
    for k in range(CX + 2 * U_EDGE):
        u_ref[k] = u_ref[k] + (1.0 / third) * a_ref[k + shift]
    up_ref[...] = u_ref[U_EDGE + 1]
    down_ref[...] = u_ref[U_EDGE + 2]
    relax_rows(a_ref, b_ref, 1, third, *gates)
    for x in range(CX):
        k = EDGE + x
        smooth_ref[x] = relax(b_ref[k - 1], b_ref[k], b_ref[k + 1], 1.0 / PROLONG)


def pool_kernel(where_ref, smooth_ref, near_ref, far_ref, send_ref, tile_ref):
    chip, core = where_ref[1], where_ref[2]
    shape = (YT, CY, CZ)
    home = lax.broadcasted_iota(jnp.int32, shape, 2) // 4
    codes = []
    for x in range(CX):
        ids = shared_ids(near_ref, far_ref, chip, core, x)
        codes.append((ids >> 6) * 3 + ((ids & 63) - home) + 1)
    pooled = []
    for half in range(2):
        parts = []
        for k in range(6):
            total = jnp.zeros(shape, F32)
            for x in range(CX):
                total = total + jnp.where(codes[x] == half * 6 + k, smooth_ref[x], 0.0)
            parts.append(jnp.sum(total, axis=1))
        pooled.append(jnp.concatenate(parts, axis=1))
    pooled = jnp.concatenate(pooled, axis=0)
    pieces = jnp.concatenate(split3(pooled), axis=0)
    sums = jnp.dot(pieces, pool_matrix(), preferred_element_type=F32)
    rows = 2 * YT
    target = sums[:rows] + sums[rows : 2 * rows] + sums[2 * rows :]
    tiles = [target[:YT], target[YT:]]
    for j in range(GY):
        tile_ref[j] = shared_tile(near_ref, far_ref, chip, core, j, CX)
    halves = [
        tile_ref[:, k, half * LANES : (half + 1) * LANES] for k in range(FIELDS) for half in range(2)
    ]
    for k in range(FIELDS):
        tiles.append(jnp.where(core == 0, halves[k], halves[FIELDS + k]))
    for i in range(GX):
        for k, tile in enumerate(tiles):
            send_ref[i, k] = tile


def solve_kernel(
    where_ref, got_ref, other_ref, near_ref, far_ref, send_ref, window_ref, ids_ref, full_ref, total_ref
):
    place, chip, core = where_ref[0], where_ref[1], where_ref[2]

    def grid(k):
        rows = []
        for x in range(NAX):
            side, at = divmod(2 * k + x % 2, FIELDS)
            rows.append(jnp.where(core == side, got_ref[x // 2, 2 + at], other_ref[x // 2, at]))
        return jnp.stack(rows, axis=0)

    coefs = with_lower(grid(0), grid(1), grid(2), grid(3))
    target = jnp.stack([got_ref[x // 2, x % 2] for x in range(NAX)], axis=0)
    pre, residual = coarse_smooth(target, coefs, True)
    for k, value in enumerate((*coefs, pre, residual)):
        full_ref[k] = value
    for k in range(10):
        for w in range(WINDOW):
            x = 2 * place + w - 4
            row = full_ref[k, jnp.clip(x, 0, NAX - 1)]
            if not 4 <= w < 6:
                row = jnp.where(jnp.logical_and(x >= 0, x < NAX), row, 1.0 if k in (0, 7) else 0.0)
            window_ref[k, w] = row
    ids = grid(4)
    full_ref[10] = ids
    for w in range(WINDOW + 2):
        ids_ref[w] = full_ref[10, jnp.clip(2 * place + w - 5, 0, NAX - 1)].astype(jnp.int32)
    ids = ids.astype(jnp.int32)
    high_of = ids >> 7
    low_of = ids & (LANES - 1)
    high_iota = lax.broadcasted_iota(jnp.int32, (HI, LANES), 0)
    low_iota = lax.broadcasted_iota(jnp.int32, (LANES, LANES), 0)
    counted = jnp.zeros((3 * HI, LANES), F32)
    for x in range(NAX):
        left, right = [], []
        for k in range(YT):
            picked = jnp.where(high_of[x, k : k + 1] == high_iota, residual[x, k : k + 1], 0.0)
            left.append(jnp.concatenate(split3(picked), axis=0))
            right.append(jnp.where(low_of[x, k : k + 1] == low_iota, 1.0, 0.0).astype(BF16))
        counted = counted + lax.dot_general(
            jnp.concatenate(left, axis=1),
            jnp.concatenate(right, axis=1),
            (((1,), (1,)), ((), ())),
            preferred_element_type=F32,
        )
    target = counted[:HI] + counted[HI : 2 * HI] + counted[2 * HI :]
    for ref, side in ((near_ref, core), (far_ref, 1 - core)):
        for k in range(4):
            total = jnp.zeros((HI, LANES), F32)
            for h in range(HI):
                total = total + ref[k, :, h * LANES : (h + 1) * LANES] * target[h : h + 1]
            at = lax.rem(chip + 4 - k, 4) * 2 + side
            total_ref[pl.ds(pl.multiple_of(at * HI, HI), HI)] = total
    row = jnp.sum(total_ref[...].T, axis=0, keepdims=True)
    tile = jnp.broadcast_to(row, (8, LANES))
    for i in range(GX):
        send_ref[i] = tile


def lane_take(table, index):
    return jnp.take_along_axis(table, index, axis=1, mode="promise_in_bounds")


def up_kernel(
    where_ref,
    table_ref,
    window_ref,
    ids_ref,
    near_ref,
    far_ref,
    u_hbm,
    ul_ref,
    ur_ref,
    out_ref,
    post_ref,
    a_ref,
    b_ref,
    u_ref,
    u_sem,
):
    u_copy = pltpu.make_async_copy(u_hbm, u_ref, u_sem)
    u_copy.start()
    place, chip, core = where_ref[0], where_ref[1], where_ref[2]
    keep_low = jnp.where(place > 0, 1.0, 0.0).astype(F32)
    keep_high = jnp.where(place < GX - 1, 1.0, 0.0).astype(F32)
    coefs = tuple(window_ref[k] for k in range(8))
    picked = []
    for w in range(WINDOW + 2):
        unknown = ids_ref[w]
        high_of = unknown >> 7
        low_of = unknown & (LANES - 1)
        value = jnp.zeros((YT, LANES), F32)
        for k in range(HI):
            table = jnp.broadcast_to(table_ref[k, 0:1], (YT, LANES))
            value = jnp.where(high_of == k, lane_take(table, low_of), value)
        picked.append(value)
    coarsest = jnp.stack(picked[1:-1], axis=0)
    rest = window_ref[9] - coarse_apply(coarsest, coefs, picked[0], picked[-1])
    update, unused = coarse_smooth(rest, coefs, False)
    post = window_ref[8] + coarsest + update
    for k in range(6):
        gate = keep_low if k < 2 else (keep_high if k >= 4 else None)
        row = post[k + 2]
        post_ref[k] = row if gate is None else row * gate

    for slab, first_tile in ((0, CX + 1), (1, 0), (2, 2 * CX + 1)):
        for x in range(CX):
            ids = shared_ids(near_ref, far_ref, chip, core, first_tile + x)
            for k in range(YT):
                table0 = jnp.broadcast_to(post_ref[2 * slab, k : k + 1], (CY, LANES))
                table1 = jnp.broadcast_to(post_ref[2 * slab + 1, k : k + 1], (CY, LANES))
                for part in range(2):
                    lanes = slice(part * LANES, (part + 1) * LANES)
                    cell = ids[k, :, lanes]
                    low = cell & (LANES - 1)
                    value = jnp.where(cell >= LANES, lane_take(table1, low), lane_take(table0, low))
                    a_ref[slab * CX + x, k, :, lanes] = value

    gates = keep_low, keep_high
    first, second, third = FINE_NODES
    u_copy.wait()
    relax_rows(a_ref, b_ref, 2, 1.0 / PROLONG, *gates, plus=u_ref)
    for k, u, gate in ((EDGE - 3, ul_ref, keep_low), (EDGE + CX + 2, ur_ref, keep_high)):
        b_ref[k] = (relax(a_ref[k - 1], a_ref[k], a_ref[k + 1], 1.0 / PROLONG) + u[...]) * gate
    relax_rows(b_ref, a_ref, 2, first, *gates)
    relax_rows(a_ref, b_ref, 1, second, *gates)
    for x in range(CX):
        k = EDGE + x
        out_ref[:, x] = relax(b_ref[k - 1], b_ref[k], b_ref[k + 1], third) + u_ref[U_EDGE + x]


def call(kernel, out_shape, scratch, flops, scalars=0, spaces=None):
    def spec(k):
        return pl.BlockSpec(memory_space=pltpu.SMEM if k < scalars else (spaces or {}).get(k, pltpu.VMEM))

    def run(*args):
        return pl.pallas_call(
            kernel,
            out_shape=out_shape,
            in_specs=[spec(k) for k in range(len(args))],
            out_specs=jax.tree.map(lambda _: pl.BlockSpec(memory_space=pltpu.VMEM), out_shape),
            scratch_shapes=scratch,
            compiler_params=pltpu.CompilerParams(vmem_limit_bytes=24 * 1024 * 1024),
            cost_estimate=pl.CostEstimate(flops=flops, bytes_accessed=2**20, transcendentals=0),
        )(*args)

    return run


def shifted(value, step):
    return lax.ppermute(value, "gx", [(k, (k + step) % GX) for k in range(GX)])


FINE_FLOPS = 3 * 10**10


def chip_below(value, step):
    return lax.ppermute(value, "gy", [(j, (j + 2 * step) % GY) for j in range(GY)])


def other_core(value):
    return lax.ppermute(value, "gy", [(j, j ^ 1) for j in range(GY)])


def local(right_side, fine_ids, coarse_diag, coarse_links, coarse_ids, coarsest_inverse):
    row = lax.axis_index("gy")
    place = jnp.stack([lax.axis_index("gx"), row // 2, row % 2]).astype(jnp.int32)
    cells = lax.all_to_all(right_side, "gy", 0, 0, tiled=True)
    low, high = shifted(cells, 1), shifted(cells, -1)

    arguments = (fine_ids, coarse_diag, coarse_links, coarse_ids)
    tiles = call(
        tiles_kernel,
        pltpu.VMEM((CX + 1, CY, CZ), F32),
        [
            pltpu.VMEM((CX, CY, CZ), jnp.int32),
            pltpu.VMEM((2, 2, 64), F32),
            pltpu.VMEM((6, 2, 2, 64), F32),
            pltpu.VMEM((2, 2, 64), jnp.int32),
            pltpu.SemaphoreType.DMA((4,)),
        ],
        10**8,
        0,
        dict.fromkeys(range(4), pltpu.HBM),
    )(*(pltpu.with_memory_space_constraint(value, pltpu.HBM) for value in arguments))
    shared = call(share_kernel, pltpu.VMEM((SHARED, CY, CZ), F32), [], 10**8)(
        tiles, shifted(tiles[:CX], 1), shifted(tiles[:CX], -1)
    )
    inverse = [coarsest_inverse, chip_below(coarsest_inverse, 1), None, chip_below(coarsest_inverse, 3)]
    shared, inverse[1], inverse[3] = lax.optimization_barrier((shared, inverse[1], inverse[3]))
    near = jnp.stack([shared, *(chip_below(shared, k) for k in range(1, 4))], axis=0)
    far = other_core(near)

    field = (ROWS, YT, CY, CZ)
    smooth, u, going_up, going_down = call(
        down_kernel,
        [
            pltpu.VMEM((CX, YT, CY, CZ), F32),
            pltpu.VMEM((CX + 2 * U_EDGE, YT, CY, CZ), F32),
            pltpu.VMEM((YT, CY, CZ), F32),
            pltpu.VMEM((YT, CY, CZ), F32),
        ],
        [pltpu.VMEM(field, F32), pltpu.VMEM(field, F32)],
        FINE_FLOPS,
        1,
    )(place, low, cells, high)
    send = call(
        pool_kernel,
        pltpu.VMEM((GX, 2 + FIELDS, YT, LANES), F32),
        [pltpu.VMEM((GY, CY, CZ), F32)],
        2 * 10**9,
        1,
    )(place, smooth, near, far)
    send, inverse[0] = lax.optimization_barrier((send, inverse[0]))
    inverse[2] = chip_below(inverse[0], 2)
    inverse_near = jnp.stack(inverse, axis=0)
    inverse_far = other_core(inverse_near)
    u_low, u_high = shifted(going_up, 1), shifted(going_down, -1)
    got = lax.all_to_all(send, "gx", 0, 0, tiled=True)
    got, u_low, u_high = lax.optimization_barrier((got, u_low, u_high))
    send, window, unknowns = call(
        solve_kernel,
        [
            pltpu.VMEM((GX, 8, LANES), F32),
            pltpu.VMEM((10, WINDOW, YT, LANES), F32),
            pltpu.VMEM((WINDOW + 2, YT, LANES), jnp.int32),
        ],
        [pltpu.VMEM((11, NAX, YT, LANES), F32), pltpu.VMEM((LANES, LANES), F32)],
        3 * 10**9,
        1,
    )(place, got, other_core(got[:, 2:]), inverse_near, inverse_far)
    table = lax.all_to_all(send, "gx", 0, 0, tiled=True)
    out = call(
        up_kernel,
        pltpu.VMEM((YT, CX, CY, CZ), F32),
        [
            pltpu.VMEM((6, YT, LANES), F32),
            pltpu.VMEM(field, F32),
            pltpu.VMEM(field, F32),
            pltpu.VMEM((CX + 2 * U_EDGE, YT, CY, CZ), F32),
            pltpu.SemaphoreType.DMA,
        ],
        4 * 10**9,
        1,
        {6: pltpu.HBM},
    )(place, table, window, unknowns, near, far, pltpu.with_memory_space_constraint(u, pltpu.HBM), u_low, u_high)
    return lax.all_to_all(out, "gy", 0, 0, tiled=True)


def solution(mesh):
    return jax.shard_map(
        local,
        mesh=mesh,
        in_specs=(
            P(None, "gx", "gy", None),
            P("gx", "gy", None),
            P("gx", "gy", None),
            P(None, "gx", "gy", None),
            P("gx", "gy", None),
            P(("gx", "gy"), None),
        ),
        out_specs=P(None, "gx", "gy", None),
        check_vma=False,
    )
```

```python
import math

import jax
import jax.numpy as jnp
from jax import lax
from jax.experimental import pallas as pl
from jax.experimental.pallas import tpu as pltpu
from jax.sharding import PartitionSpec as P

F32 = jnp.float32
BF16 = jnp.bfloat16

PROLONG = 1.0 / 9.0


def nodes(low, high):
    theta = (high + low) / 2.0
    delta = (high - low) / 2.0
    reach = delta * math.cos(math.pi / 6.0)
    return (theta + reach, theta - reach, theta)


FINE_NODES = tuple(6.0 * node for node in nodes(2.0 / 30.0, 2.0))
COARSE_NODES = nodes(0.19, 1.9)

RHS, CX, YT, CY, CZ = 8, 4, 8, 8, 256
GX, GY = 16, 8
LANES = 128
NC2 = 2048
HI = NC2 // LANES
HALF = LANES // 2


def beside_in_row(row):
    sub = lax.broadcasted_iota(jnp.int32, row.shape, 1)
    lane = lax.broadcasted_iota(jnp.int32, row.shape, 2)
    zero_tile = jnp.zeros((1,) + row.shape[1:], F32)
    up = pltpu.roll(row, 1, 1)
    up = jnp.where(sub == 0, jnp.concatenate([zero_tile, up[:-1]], axis=0), up)
    down = pltpu.roll(row, CY - 1, 1)
    down = jnp.where(sub == CY - 1, jnp.concatenate([down[1:], zero_tile], axis=0), down)
    left = jnp.where(lane == 0, 0.0, pltpu.roll(row, 1, 2))
    right = jnp.where(lane == CZ - 1, 0.0, pltpu.roll(row, CZ - 1, 2))
    return (up + down) + (left + right)


def relax(low, row, high, node):
    return (1.0 - 6.0 / node) * row + (1.0 / node) * (low + high + beside_in_row(row))


def beside_grid(grid):
    sub = lax.broadcasted_iota(jnp.int32, grid.shape, 1)
    lane = lax.broadcasted_iota(jnp.int32, grid.shape, 2)
    turned = pltpu.roll(grid, LANES // 2, 2)
    low_y = jnp.where(lane < LANES // 2, pltpu.roll(turned, 1, 1), turned)
    high_y = jnp.where(lane < LANES // 2, turned, pltpu.roll(turned, YT - 1, 1))
    low_z = pltpu.roll(grid, 1, 2)
    high_z = pltpu.roll(grid, LANES - 1, 2)
    del sub
    return low_y, high_y, low_z, high_z


def lower_of(grid):
    return jnp.concatenate([jnp.zeros((1,) + grid.shape[1:], F32), grid[:-1]], axis=0)


def upper_of(grid):
    return jnp.concatenate([grid[1:], jnp.zeros((1,) + grid.shape[1:], F32)], axis=0)


NAX = 2 * GX
WINDOW = 10
FIELDS = 5


def with_lower(diag, ux, uy, uz):
    return (diag, lower_of(ux), ux, beside_grid(uy)[0], uy, beside_grid(uz)[2], uz, 1.0 / diag)


def coarse_apply(grid, coefs, below=None, above=None):
    diag, lx, ux, ly, uy, lz, uz = coefs[:7]
    low_y, high_y, low_z, high_z = beside_grid(grid)
    low_x = lower_of(grid) if below is None else jnp.concatenate([below[None], grid[:-1]], axis=0)
    high_x = upper_of(grid) if above is None else jnp.concatenate([grid[1:], above[None]], axis=0)
    linked = lx * low_x + ux * high_x
    linked = linked + ly * low_y + uy * high_y
    linked = linked + lz * low_z + uz * high_z
    return diag * grid - linked


def coarse_smooth(residual, coefs, with_last):
    total = None
    for k, node in enumerate(COARSE_NODES):
        update = (1.0 / node) * coefs[7] * residual
        total = update if total is None else total + update
        if k < 2 or with_last:
            residual = residual - coarse_apply(update, coefs)
    return total, residual


def split3(value):
    first = value.astype(BF16)
    rest = value - first.astype(F32)
    second = rest.astype(BF16)
    third = (rest - second.astype(F32)).astype(BF16)
    return first, second, third


def tiles_kernel(ids_ref, diag_ref, links_ref, coarse_ids_ref, out_ref, id_buf, diag_buf, link_buf, cid_buf, sems):
    pairs = ((ids_ref, id_buf), (diag_ref, diag_buf), (links_ref, link_buf), (coarse_ids_ref, cid_buf))
    copies = [pltpu.make_async_copy(src, dst, sems.at[k]) for k, (src, dst) in enumerate(pairs)]
    for copy in copies:
        copy.start()
    for copy in copies:
        copy.wait()
    fields = (
        diag_buf[...],
        link_buf[1],
        link_buf[3],
        link_buf[5],
        cid_buf[...].astype(F32),
    )
    rows = [
        jnp.concatenate([field[half, k : k + 1] for half in range(2) for k in range(2)], axis=1)
        for field in fields
    ]
    rows.append(jnp.zeros((3, CZ), F32))
    for x in range(CX):
        out_ref[x] = id_buf[x].astype(F32)
    out_ref[CX] = jnp.concatenate(rows, axis=0)


def shared_tile(near_ref, far_ref, chip, core, j, tile):
    k = lax.rem(chip + 4 - j // 2, 4)
    return jnp.where(core == j % 2, near_ref[k, tile], far_ref[k, tile])


def shared_ids(near_ref, far_ref, chip, core, tile):
    rows = [shared_tile(near_ref, far_ref, chip, core, j, tile) for j in range(GY)]
    return jnp.stack(rows, axis=0).astype(jnp.int32)


def pool_matrix():
    lane = lax.broadcasted_iota(jnp.int32, (CZ, LANES), 1)
    gap = lane - lax.broadcasted_iota(jnp.int32, (CZ, LANES), 0) // 4
    parts = []
    for half in range(2):
        for shift in range(-1, 2):
            hit = jnp.logical_and(gap == half * 64 + shift, lane // 64 == half)
            parts.append(jnp.where(hit, 1.0, 0.0).astype(BF16))
    return jnp.concatenate(parts, axis=0)


EDGE = 4
ROWS = CX + 2 * EDGE
U_EDGE = 2


def relax_rows(src, dst, reach, node, keep_low, keep_high, plus=None):
    for k in range(EDGE - reach, EDGE + CX + reach):
        row = relax(src[k - 1], src[k], src[k + 1], node)
        if k < EDGE:
            row = row * keep_low
        elif k >= EDGE + CX:
            row = row * keep_high
        dst[k] = row if plus is None else row + plus[k - EDGE + U_EDGE]


def down_kernel(where_ref, t1_ref, to_ref, t2_ref, far_ref, smooth_ref, u_ref, a_ref, b_ref):
    del far_ref
    place = where_ref[0]
    odd = place & 1
    keep_low = jnp.where(place > 0, 1.0, 0.0).astype(F32)
    keep_high = jnp.where(place < GX - 1, 1.0, 0.0).astype(F32)
    gates = keep_low, keep_high
    first, second, third = FINE_NODES
    for x in range(CX):
        a_ref[x] = jnp.where(odd == 1, t1_ref[:, x], t2_ref[:, x]) * keep_low
        a_ref[EDGE + x] = to_ref[:, x]
        a_ref[EDGE + CX + x] = jnp.where(odd == 1, t2_ref[:, x], t1_ref[:, x]) * keep_high

    relax_rows(a_ref, b_ref, 3, first, *gates)
    shift = EDGE - U_EDGE
    for k in range(CX + 2 * U_EDGE):
        u_ref[k] = (1.0 / first) * a_ref[k + shift] + (1.0 / second) * b_ref[k + shift]
    relax_rows(b_ref, a_ref, 2, second, *gates)
    for k in range(CX + 2 * U_EDGE):
        u_ref[k] = u_ref[k] + (1.0 / third) * a_ref[k + shift]
    relax_rows(a_ref, b_ref, 1, third, *gates)
    for x in range(CX):
        k = EDGE + x
        smooth_ref[x] = relax(b_ref[k - 1], b_ref[k], b_ref[k + 1], 1.0 / PROLONG)


def pool_kernel(where_ref, smooth_ref, u_ref, near_ref, far_ref, send_ref, first_ref, second_ref, tile_ref):
    chip, core = where_ref[1], where_ref[2]
    shape = (YT, CY, CZ)
    home = lax.broadcasted_iota(jnp.int32, shape, 2) // 4
    codes = []
    for x in range(CX):
        ids = shared_ids(near_ref, far_ref, chip, core, x)
        first_ref[:, x] = ids.astype(F32)
        second_ref[:, x] = ids.astype(F32)
        codes.append((ids >> 6) * 3 + ((ids & 63) - home) + 1)
    odd = where_ref[0] & 1
    first_ref[:, CX] = u_ref[U_EDGE + 1 + odd]
    second_ref[:, CX] = u_ref[U_EDGE + 2 - odd]
    pooled = []
    for half in range(2):
        parts = []
        for k in range(6):
            total = jnp.zeros(shape, F32)
            for x in range(CX):
                total = total + jnp.where(codes[x] == half * 6 + k, smooth_ref[x], 0.0)
            parts.append(jnp.sum(total, axis=1))
        pooled.append(jnp.concatenate(parts, axis=1))
    pooled = jnp.concatenate(pooled, axis=0)
    pieces = jnp.concatenate(split3(pooled), axis=0)
    sums = jnp.dot(pieces, pool_matrix(), preferred_element_type=F32)
    rows = 2 * YT
    target = sums[:rows] + sums[rows : 2 * rows] + sums[2 * rows :]
    tiles = [target[:YT], target[YT:]]
    for j in range(GY):
        tile_ref[j] = shared_tile(near_ref, far_ref, chip, core, j, CX)
    halves = [
        tile_ref[:, k, half * LANES : (half + 1) * LANES] for k in range(FIELDS) for half in range(2)
    ]
    for k in range(FIELDS):
        tiles.append(jnp.where(core == 0, halves[k], halves[FIELDS + k]))
    for i in range(GX):
        for k, tile in enumerate(tiles):
            send_ref[i, k] = tile


def solve_kernel(
    where_ref, got_ref, other_ref, near_ref, far_ref, arrived_ref, send_ref, window_ref, ids_ref, full_ref, total_ref
):
    del arrived_ref

    place, chip, core = where_ref[0], where_ref[1], where_ref[2]

    def grid(k):
        rows = []
        for x in range(NAX):
            side, at = divmod(2 * k + x % 2, FIELDS)
            rows.append(jnp.where(core == side, got_ref[x // 2, 2 + at], other_ref[x // 2, at]))
        return jnp.stack(rows, axis=0)

    coefs = with_lower(grid(0), grid(1), grid(2), grid(3))
    target = jnp.stack([got_ref[x // 2, x % 2] for x in range(NAX)], axis=0)
    pre, residual = coarse_smooth(target, coefs, True)
    for k, value in enumerate((*coefs, pre, residual)):
        full_ref[k] = value
    for k in range(10):
        for w in range(WINDOW):
            x = 2 * place + w - 4
            row = full_ref[k, jnp.clip(x, 0, NAX - 1)]
            if not 4 <= w < 6:
                row = jnp.where(jnp.logical_and(x >= 0, x < NAX), row, 1.0 if k in (0, 7) else 0.0)
            window_ref[k, w] = row
    ids = grid(4)
    full_ref[10] = ids
    for w in range(WINDOW + 2):
        ids_ref[w] = full_ref[10, jnp.clip(2 * place + w - 5, 0, NAX - 1)].astype(jnp.int32)
    ids = ids.astype(jnp.int32)
    high_of = ids >> 6
    low_of = ids & (HALF - 1)
    high_iota = lax.broadcasted_iota(jnp.int32, (NC2 // HALF, LANES), 0)
    low_iota = lax.broadcasted_iota(jnp.int32, (HALF, LANES), 0)
    pieces = [piece.astype(F32) for piece in split3(residual)[:2]]
    counted = jnp.zeros((2 * NC2 // HALF, HALF), F32)
    for x in range(NAX):
        left, right = [], []
        for k in range(YT):
            hit = high_of[x, k : k + 1] == high_iota
            left.append(
                jnp.concatenate([jnp.where(hit, piece[x, k : k + 1], 0.0).astype(BF16) for piece in pieces], axis=0)
            )
            right.append(jnp.where(low_of[x, k : k + 1] == low_iota, 1.0, 0.0).astype(BF16))
        counted = counted + lax.dot_general(
            jnp.concatenate(left, axis=1),
            jnp.concatenate(right, axis=1),
            (((1,), (1,)), ((), ())),
            preferred_element_type=F32,
        )
    rows = NC2 // HALF
    target = sum(counted[k * rows : (k + 1) * rows] for k in range(2))
    target = [jnp.concatenate([target[2 * h : 2 * h + 1], target[2 * h + 1 : 2 * h + 2]], axis=1) for h in range(HI)]
    for ref, side in ((near_ref, core), (far_ref, 1 - core)):
        for k in range(4):
            total = jnp.zeros((HI, LANES), F32)
            for h in range(HI):
                total = total + ref[k, :, h * LANES : (h + 1) * LANES] * target[h]
            at = lax.rem(chip + 4 - k, 4) * 2 + side
            total_ref[pl.ds(pl.multiple_of(at * HI, HI), HI)] = total
    row = jnp.sum(total_ref[...].T, axis=0, keepdims=True)
    for i in range(GX):
        send_ref[i] = row


def lane_take(table, index):
    return jnp.take_along_axis(table, index, axis=1, mode="promise_in_bounds")


def up_kernel(
    where_ref,
    table_ref,
    window_ref,
    ids_ref,
    near_ref,
    far_ref,
    first_ref,
    second_ref,
    u_hbm,
    out_ref,
    post_ref,
    a_ref,
    b_ref,
    u_ref,
    u_sem,
):
    u_copy = pltpu.make_async_copy(u_hbm, u_ref, u_sem)
    u_copy.start()
    place, chip, core = where_ref[0], where_ref[1], where_ref[2]
    keep_low = jnp.where(place > 0, 1.0, 0.0).astype(F32)
    keep_high = jnp.where(place < GX - 1, 1.0, 0.0).astype(F32)
    coefs = tuple(window_ref[k] for k in range(8))
    picked = []
    for w in range(WINDOW + 2):
        unknown = ids_ref[w]
        high_of = unknown >> 7
        low_of = unknown & (LANES - 1)
        value = jnp.zeros((YT, LANES), F32)
        for k in range(HI):
            table = jnp.broadcast_to(table_ref[k], (YT, LANES))
            value = jnp.where(high_of == k, lane_take(table, low_of), value)
        picked.append(value)
    coarsest = jnp.stack(picked[1:-1], axis=0)
    rest = window_ref[9] - coarse_apply(coarsest, coefs, picked[0], picked[-1])
    update, unused = coarse_smooth(rest, coefs, False)
    post = window_ref[8] + coarsest + update
    for k in range(6):
        gate = keep_low if k < 2 else (keep_high if k >= 4 else None)
        row = post[k + 2]
        post_ref[k] = row if gate is None else row * gate

    odd = place & 1

    def halo(slab, x):
        first, second = first_ref[:, x], second_ref[:, x]
        return jnp.where(odd == 1, first, second) if slab == 0 else jnp.where(odd == 1, second, first)

    for slab in range(3):
        for x in range(CX):
            ids = shared_ids(near_ref, far_ref, chip, core, x) if slab == 1 else halo(slab, x).astype(jnp.int32)
            for k in range(YT):
                table0 = jnp.broadcast_to(post_ref[2 * slab, k : k + 1], (CY, LANES))
                table1 = jnp.broadcast_to(post_ref[2 * slab + 1, k : k + 1], (CY, LANES))
                for part in range(2):
                    lanes = slice(part * LANES, (part + 1) * LANES)
                    cell = ids[k, :, lanes]
                    low = cell & (LANES - 1)
                    value = jnp.where(cell >= LANES, lane_take(table1, low), lane_take(table0, low))
                    a_ref[slab * CX + x, k, :, lanes] = value

    gates = keep_low, keep_high
    first, second, third = FINE_NODES
    u_copy.wait()
    relax_rows(a_ref, b_ref, 2, 1.0 / PROLONG, *gates, plus=u_ref)
    for k, slab, gate in ((EDGE - 3, 0, keep_low), (EDGE + CX + 2, 2, keep_high)):
        b_ref[k] = (relax(a_ref[k - 1], a_ref[k], a_ref[k + 1], 1.0 / PROLONG) + halo(slab, CX)) * gate
    relax_rows(b_ref, a_ref, 2, first, *gates)
    relax_rows(a_ref, b_ref, 1, second, *gates)
    for x in range(CX):
        k = EDGE + x
        out_ref[:, x] = relax(b_ref[k - 1], b_ref[k], b_ref[k + 1], third) + u_ref[U_EDGE + x]


def call(kernel, out_shape, scratch, flops, scalars=0, spaces=None):
    def spec(k):
        return pl.BlockSpec(memory_space=pltpu.SMEM if k < scalars else (spaces or {}).get(k, pltpu.VMEM))

    def run(*args):
        return pl.pallas_call(
            kernel,
            out_shape=out_shape,
            in_specs=[spec(k) for k in range(len(args))],
            out_specs=jax.tree.map(lambda _: pl.BlockSpec(memory_space=pltpu.VMEM), out_shape),
            scratch_shapes=scratch,
            compiler_params=pltpu.CompilerParams(vmem_limit_bytes=24 * 1024 * 1024),
            cost_estimate=pl.CostEstimate(flops=flops, bytes_accessed=2**20, transcendentals=0),
        )(*args)

    return run


def beside(first, second):
    one = [(k, k ^ 1) for k in range(GX)]
    two = [(k, ((k + 1) ^ 1) - 1) for k in range(GX)]
    two = [(k, other % GX) for k, other in two]
    return lax.ppermute(first, "gx", one), lax.ppermute(second, "gx", two)


FINE_FLOPS = 3 * 10**10


def chip_below(value, step):
    return lax.ppermute(value, "gy", [(j, (j + 2 * step) % GY) for j in range(GY)])


def arrived_kernel(low_ref, high_ref, out_ref):
    out_ref[...] = low_ref[0, CX, :, :LANES] + high_ref[0, CX, :, :LANES]


def other_core(value):
    return lax.ppermute(value, "gy", [(j, j ^ 1) for j in range(GY)])


def local(right_side, fine_ids, coarse_diag, coarse_links, coarse_ids, coarsest_inverse):
    row = lax.axis_index("gy")
    place = jnp.stack([lax.axis_index("gx"), row // 2, row % 2]).astype(jnp.int32)
    cells = lax.all_to_all(right_side, "gy", 0, 0, tiled=True)

    arguments = (fine_ids, coarse_diag, coarse_links, coarse_ids)
    tiles = call(
        tiles_kernel,
        pltpu.VMEM((CX + 1, CY, CZ), F32),
        [
            pltpu.VMEM((CX, CY, CZ), jnp.int32),
            pltpu.VMEM((2, 2, 64), F32),
            pltpu.VMEM((6, 2, 2, 64), F32),
            pltpu.VMEM((2, 2, 64), jnp.int32),
            pltpu.SemaphoreType.DMA((4,)),
        ],
        10**8,
        0,
        dict.fromkeys(range(4), pltpu.HBM),
    )(*(pltpu.with_memory_space_constraint(value, pltpu.HBM) for value in arguments))
    slabs = [tiles, *(chip_below(tiles, k) for k in range(1, 4))]
    cells, *slabs = lax.optimization_barrier((cells, *slabs))
    near = jnp.stack(slabs, axis=0)
    far = other_core(near)

    first, second = beside(cells, cells)

    cells, inverse = lax.optimization_barrier((cells, coarsest_inverse))
    chips = [chip_below(inverse, k) for k in range(1, 4)]

    field = (ROWS, YT, CY, CZ)
    smooth, u = call(
        down_kernel,
        [
            pltpu.VMEM((CX, YT, CY, CZ), F32),
            pltpu.VMEM((CX + 2 * U_EDGE, YT, CY, CZ), F32),
        ],
        [pltpu.VMEM(field, F32), pltpu.VMEM(field, F32)],
        FINE_FLOPS,
        1,
    )(place, first, cells, second, far)
    send, *going = call(
        pool_kernel,
        [
            pltpu.VMEM((GX, 2 + FIELDS, YT, LANES), F32),
            pltpu.VMEM((YT, CX + 1, CY, CZ), F32),
            pltpu.VMEM((YT, CX + 1, CY, CZ), F32),
        ],
        [pltpu.VMEM((GY, CY, CZ), F32)],
        2 * 10**9,
        1,
    )(place, smooth, u, near, far)
    send, inverse, *chips = lax.optimization_barrier((send, inverse, *chips))
    inverse_near = jnp.stack([inverse, *chips], axis=0)
    inverse_far = other_core(inverse_near)
    first, second = beside(*going)
    got = lax.all_to_all(send, "gx", 0, 0, tiled=True)
    arrived = call(arrived_kernel, pltpu.VMEM((CY, LANES), F32), [], 2 * 10**10)(first, second)
    got, arrived = lax.optimization_barrier((got, arrived))
    send, window, unknowns = call(
        solve_kernel,
        [
            pltpu.VMEM((GX, 1, LANES), F32),
            pltpu.VMEM((10, WINDOW, YT, LANES), F32),
            pltpu.VMEM((WINDOW + 2, YT, LANES), jnp.int32),
        ],
        [pltpu.VMEM((11, NAX, YT, LANES), F32), pltpu.VMEM((LANES, LANES), F32)],
        10**6,
        1,
    )(place, got, other_core(got[:, 2:]), inverse_near, inverse_far, arrived)
    table = lax.all_to_all(send, "gx", 0, 0, tiled=True)
    out = call(
        up_kernel,
        pltpu.VMEM((YT, CX, CY, CZ), F32),
        [
            pltpu.VMEM((6, YT, LANES), F32),
            pltpu.VMEM(field, F32),
            pltpu.VMEM(field, F32),
            pltpu.VMEM((CX + 2 * U_EDGE, YT, CY, CZ), F32),
            pltpu.SemaphoreType.DMA,
        ],
        4 * 10**9,
        1,
        {8: pltpu.HBM},
    )(place, table, window, unknowns, near, far, first, second, pltpu.with_memory_space_constraint(u, pltpu.HBM))
    return lax.all_to_all(out, "gy", 0, 0, tiled=True)


def solution(mesh):
    return jax.shard_map(
        local,
        mesh=mesh,
        in_specs=(
            P(None, "gx", "gy", None),
            P("gx", "gy", None),
            P("gx", "gy", None),
            P(None, "gx", "gy", None),
            P("gx", "gy", None),
            P(("gx", "gy"), None),
        ),
        out_specs=P(None, "gx", "gy", None),
        check_vma=False,
    )
```

```python
import math

import jax
import jax.numpy as jnp
from jax import lax
from jax.experimental import pallas as pl
from jax.experimental.pallas import tpu as pltpu
from jax.sharding import PartitionSpec as P

F32 = jnp.float32
BF16 = jnp.bfloat16

PROLONG = 1.0 / 9.0


def nodes(low, high):
    theta = (high + low) / 2.0
    delta = (high - low) / 2.0
    reach = delta * math.cos(math.pi / 6.0)
    return (theta + reach, theta - reach, theta)


FINE_NODES = tuple(6.0 * node for node in nodes(2.0 / 30.0, 2.0))
COARSE_NODES = nodes(0.19, 1.9)

RHS, CX, YT, CY, CZ = 8, 4, 8, 8, 256
GX, GY = 16, 8
LANES = 128
NC2 = 2048
HI = NC2 // LANES
HALF = LANES // 2


def beside_in_row(row):
    sub = lax.broadcasted_iota(jnp.int32, row.shape, 1)
    lane = lax.broadcasted_iota(jnp.int32, row.shape, 2)
    zero_tile = jnp.zeros((1,) + row.shape[1:], F32)
    up = pltpu.roll(row, 1, 1)
    up = jnp.where(sub == 0, jnp.concatenate([zero_tile, up[:-1]], axis=0), up)
    down = pltpu.roll(row, CY - 1, 1)
    down = jnp.where(sub == CY - 1, jnp.concatenate([down[1:], zero_tile], axis=0), down)
    left = jnp.where(lane == 0, 0.0, pltpu.roll(row, 1, 2))
    right = jnp.where(lane == CZ - 1, 0.0, pltpu.roll(row, CZ - 1, 2))
    return (up + down) + (left + right)


def relax(low, row, high, node):
    return (1.0 - 6.0 / node) * row + (1.0 / node) * (low + high + beside_in_row(row))


def beside_grid(grid):
    sub = lax.broadcasted_iota(jnp.int32, grid.shape, 1)
    lane = lax.broadcasted_iota(jnp.int32, grid.shape, 2)
    turned = pltpu.roll(grid, LANES // 2, 2)
    low_y = jnp.where(lane < LANES // 2, pltpu.roll(turned, 1, 1), turned)
    high_y = jnp.where(lane < LANES // 2, turned, pltpu.roll(turned, YT - 1, 1))
    low_z = pltpu.roll(grid, 1, 2)
    high_z = pltpu.roll(grid, LANES - 1, 2)
    del sub
    return low_y, high_y, low_z, high_z


def lower_of(grid):
    return jnp.concatenate([jnp.zeros((1,) + grid.shape[1:], F32), grid[:-1]], axis=0)


def upper_of(grid):
    return jnp.concatenate([grid[1:], jnp.zeros((1,) + grid.shape[1:], F32)], axis=0)


NAX = 2 * GX
WINDOW = 10
FIELDS = 5


def with_lower(diag, ux, uy, uz):
    return (diag, lower_of(ux), ux, beside_grid(uy)[0], uy, beside_grid(uz)[2], uz, 1.0 / diag)


def coarse_apply(grid, coefs, below=None, above=None):
    diag, lx, ux, ly, uy, lz, uz = coefs[:7]
    low_y, high_y, low_z, high_z = beside_grid(grid)
    low_x = lower_of(grid) if below is None else jnp.concatenate([below[None], grid[:-1]], axis=0)
    high_x = upper_of(grid) if above is None else jnp.concatenate([grid[1:], above[None]], axis=0)
    linked = lx * low_x + ux * high_x
    linked = linked + ly * low_y + uy * high_y
    linked = linked + lz * low_z + uz * high_z
    return diag * grid - linked


def coarse_smooth(residual, coefs, with_last):
    total = None
    for k, node in enumerate(COARSE_NODES):
        update = (1.0 / node) * coefs[7] * residual
        total = update if total is None else total + update
        if k < 2 or with_last:
            residual = residual - coarse_apply(update, coefs)
    return total, residual


def split3(value):
    first = value.astype(BF16)
    rest = value - first.astype(F32)
    second = rest.astype(BF16)
    third = (rest - second.astype(F32)).astype(BF16)
    return first, second, third


def tiles_kernel(ids_ref, diag_ref, links_ref, coarse_ids_ref, out_ref, id_buf, diag_buf, link_buf, cid_buf, sems):
    pairs = ((ids_ref, id_buf), (diag_ref, diag_buf), (links_ref, link_buf), (coarse_ids_ref, cid_buf))
    copies = [pltpu.make_async_copy(src, dst, sems.at[k]) for k, (src, dst) in enumerate(pairs)]
    for copy in copies:
        copy.start()
    for copy in copies:
        copy.wait()
    fields = (
        diag_buf[...],
        link_buf[1],
        link_buf[3],
        link_buf[5],
        cid_buf[...].astype(F32),
    )
    rows = [
        jnp.concatenate([field[half, k : k + 1] for half in range(2) for k in range(2)], axis=1)
        for field in fields
    ]
    rows.append(jnp.zeros((3, CZ), F32))
    for x in range(CX):
        out_ref[x] = id_buf[x].astype(F32)
    out_ref[CX] = jnp.concatenate(rows, axis=0)


def shared_tile(near_ref, far_ref, chip, core, j, tile):
    k = lax.rem(chip + 4 - j // 2, 4)
    return jnp.where(core == j % 2, near_ref[k, tile], far_ref[k, tile])


def shared_ids(near_ref, far_ref, chip, core, tile):
    rows = [shared_tile(near_ref, far_ref, chip, core, j, tile) for j in range(GY)]
    return jnp.stack(rows, axis=0).astype(jnp.int32)


def pool_matrix():
    lane = lax.broadcasted_iota(jnp.int32, (CZ, LANES), 1)
    gap = lane - lax.broadcasted_iota(jnp.int32, (CZ, LANES), 0) // 4
    parts = []
    for half in range(2):
        for shift in range(-1, 2):
            hit = jnp.logical_and(gap == half * 64 + shift, lane // 64 == half)
            parts.append(jnp.where(hit, 1.0, 0.0).astype(BF16))
    return jnp.concatenate(parts, axis=0)


EDGE = 4
ROWS = CX + 2 * EDGE
U_EDGE = 2


def relax_rows(src, dst, reach, node, keep_low, keep_high, plus=None):
    for k in range(EDGE - reach, EDGE + CX + reach):
        row = relax(src[k - 1], src[k], src[k + 1], node)
        if k < EDGE:
            row = row * keep_low
        elif k >= EDGE + CX:
            row = row * keep_high
        dst[k] = row if plus is None else row + plus[k - EDGE + U_EDGE]


def down_kernel(
    where_ref,
    t1_ref,
    to_ref,
    t2_ref,
    near_ref,
    far_ref,
    send_ref,
    first_ref,
    second_ref,
    u_hbm,
    a_ref,
    b_ref,
    tile_ref,
    u_ref,
    u_sem,
):
    place, chip, core = where_ref[0], where_ref[1], where_ref[2]
    odd = place & 1
    keep_low = jnp.where(place > 0, 1.0, 0.0).astype(F32)
    keep_high = jnp.where(place < GX - 1, 1.0, 0.0).astype(F32)
    gates = keep_low, keep_high
    first, second, third = FINE_NODES
    for x in range(CX):
        a_ref[x] = jnp.where(odd == 1, t1_ref[:, x], t2_ref[:, x]) * keep_low
        a_ref[EDGE + x] = to_ref[:, x]
        a_ref[EDGE + CX + x] = jnp.where(odd == 1, t2_ref[:, x], t1_ref[:, x]) * keep_high

    relax_rows(a_ref, b_ref, 3, first, *gates)
    shift = EDGE - U_EDGE
    for k in range(CX + 2 * U_EDGE):
        u_ref[k] = (1.0 / first) * a_ref[k + shift] + (1.0 / second) * b_ref[k + shift]
    relax_rows(b_ref, a_ref, 2, second, *gates)
    for k in range(CX + 2 * U_EDGE):
        u_ref[k] = u_ref[k] + (1.0 / third) * a_ref[k + shift]
    u_copy = pltpu.make_async_copy(u_ref, u_hbm, u_sem)
    u_copy.start()
    relax_rows(a_ref, b_ref, 1, third, *gates)
    smooth = []
    for x in range(CX):
        k = EDGE + x
        smooth.append(relax(b_ref[k - 1], b_ref[k], b_ref[k + 1], 1.0 / PROLONG))

    shape = (YT, CY, CZ)
    home = lax.broadcasted_iota(jnp.int32, shape, 2) // 4
    codes = []
    for x in range(CX):
        ids = shared_ids(near_ref, far_ref, chip, core, x)
        first_ref[:, x] = ids.astype(F32)
        second_ref[:, x] = ids.astype(F32)
        codes.append((ids >> 6) * 3 + ((ids & 63) - home) + 1)
    first_ref[:, CX] = u_ref[U_EDGE + 1 + odd]
    second_ref[:, CX] = u_ref[U_EDGE + 2 - odd]
    pooled = []
    for half in range(2):
        parts = []
        for k in range(6):
            total = jnp.zeros(shape, F32)
            for x in range(CX):
                total = total + jnp.where(codes[x] == half * 6 + k, smooth[x], 0.0)
            parts.append(jnp.sum(total, axis=1))
        pooled.append(jnp.concatenate(parts, axis=1))
    pooled = jnp.concatenate(pooled, axis=0)
    pieces = jnp.concatenate(split3(pooled), axis=0)
    sums = jnp.dot(pieces, pool_matrix(), preferred_element_type=F32)
    rows = 2 * YT
    target = sums[:rows] + sums[rows : 2 * rows] + sums[2 * rows :]
    tiles = [target[:YT], target[YT:]]
    for j in range(GY):
        tile_ref[j] = shared_tile(near_ref, far_ref, chip, core, j, CX)
    halves = [
        tile_ref[:, k, half * LANES : (half + 1) * LANES] for k in range(FIELDS) for half in range(2)
    ]
    for k in range(FIELDS):
        tiles.append(jnp.where(core == 0, halves[k], halves[FIELDS + k]))
    for i in range(GX):
        for k, tile in enumerate(tiles):
            send_ref[i, k] = tile
    u_copy.wait()


def solve_kernel(
    where_ref, got_ref, other_ref, near_ref, far_ref, arrived_ref, send_ref, window_ref, ids_ref, full_ref, total_ref
):
    del arrived_ref

    place, chip, core = where_ref[0], where_ref[1], where_ref[2]

    def grid(k):
        rows = []
        for x in range(NAX):
            side, at = divmod(2 * k + x % 2, FIELDS)
            rows.append(jnp.where(core == side, got_ref[x // 2, 2 + at], other_ref[x // 2, at]))
        return jnp.stack(rows, axis=0)

    coefs = with_lower(grid(0), grid(1), grid(2), grid(3))
    target = jnp.stack([got_ref[x // 2, x % 2] for x in range(NAX)], axis=0)
    pre, residual = coarse_smooth(target, coefs, True)
    for k, value in enumerate((*coefs, pre, residual)):
        full_ref[k] = value
    for k in range(10):
        for w in range(WINDOW):
            x = 2 * place + w - 4
            row = full_ref[k, jnp.clip(x, 0, NAX - 1)]
            if not 4 <= w < 6:
                row = jnp.where(jnp.logical_and(x >= 0, x < NAX), row, 1.0 if k in (0, 7) else 0.0)
            window_ref[k, w] = row
    ids = grid(4)
    full_ref[10] = ids
    for w in range(WINDOW + 2):
        ids_ref[w] = full_ref[10, jnp.clip(2 * place + w - 5, 0, NAX - 1)].astype(jnp.int32)
    ids = ids.astype(jnp.int32)
    high_of = ids >> 6
    low_of = ids & (HALF - 1)
    high_iota = lax.broadcasted_iota(jnp.int32, (NC2 // HALF, LANES), 0)
    low_iota = lax.broadcasted_iota(jnp.int32, (HALF, LANES), 0)
    pieces = [piece.astype(F32) for piece in split3(residual)[:2]]
    counted = jnp.zeros((2 * NC2 // HALF, HALF), F32)
    for x in range(NAX):
        left, right = [], []
        for k in range(YT):
            hit = high_of[x, k : k + 1] == high_iota
            left.append(
                jnp.concatenate([jnp.where(hit, piece[x, k : k + 1], 0.0).astype(BF16) for piece in pieces], axis=0)
            )
            right.append(jnp.where(low_of[x, k : k + 1] == low_iota, 1.0, 0.0).astype(BF16))
        counted = counted + lax.dot_general(
            jnp.concatenate(left, axis=1),
            jnp.concatenate(right, axis=1),
            (((1,), (1,)), ((), ())),
            preferred_element_type=F32,
        )
    rows = NC2 // HALF
    target = sum(counted[k * rows : (k + 1) * rows] for k in range(2))
    target = [jnp.concatenate([target[2 * h : 2 * h + 1], target[2 * h + 1 : 2 * h + 2]], axis=1) for h in range(HI)]
    for ref, side in ((near_ref, core), (far_ref, 1 - core)):
        for k in range(4):
            total = jnp.zeros((HI, LANES), F32)
            for h in range(HI):
                total = total + ref[k, :, h * LANES : (h + 1) * LANES] * target[h]
            at = lax.rem(chip + 4 - k, 4) * 2 + side
            total_ref[pl.ds(pl.multiple_of(at * HI, HI), HI)] = total
    row = jnp.sum(total_ref[...].T, axis=0, keepdims=True)
    for i in range(GX):
        send_ref[i] = row


def lane_take(table, index):
    return jnp.take_along_axis(table, index, axis=1, mode="promise_in_bounds")


def up_kernel(
    where_ref,
    table_ref,
    window_ref,
    ids_ref,
    own_ref,
    first_ref,
    second_ref,
    u_hbm,
    out_ref,
    post_ref,
    a_ref,
    b_ref,
    u_ref,
    u_sem,
):
    u_copy = pltpu.make_async_copy(u_hbm, u_ref, u_sem)
    u_copy.start()
    place = where_ref[0]
    keep_low = jnp.where(place > 0, 1.0, 0.0).astype(F32)
    keep_high = jnp.where(place < GX - 1, 1.0, 0.0).astype(F32)
    coefs = tuple(window_ref[k] for k in range(8))
    picked = []
    for w in range(WINDOW + 2):
        unknown = ids_ref[w]
        high_of = unknown >> 7
        low_of = unknown & (LANES - 1)
        value = jnp.zeros((YT, LANES), F32)
        for k in range(HI):
            table = jnp.broadcast_to(table_ref[k], (YT, LANES))
            value = jnp.where(high_of == k, lane_take(table, low_of), value)
        picked.append(value)
    coarsest = jnp.stack(picked[1:-1], axis=0)
    rest = window_ref[9] - coarse_apply(coarsest, coefs, picked[0], picked[-1])
    update, unused = coarse_smooth(rest, coefs, False)
    post = window_ref[8] + coarsest + update
    for k in range(6):
        gate = keep_low if k < 2 else (keep_high if k >= 4 else None)
        row = post[k + 2]
        post_ref[k] = row if gate is None else row * gate

    odd = place & 1

    def halo(slab, x):
        first, second = first_ref[:, x], second_ref[:, x]
        return jnp.where(odd == 1, first, second) if slab == 0 else jnp.where(odd == 1, second, first)

    for slab in range(3):
        for x in range(CX):
            ids = (own_ref[:, x] if slab == 1 else halo(slab, x)).astype(jnp.int32)
            for k in range(YT):
                table0 = jnp.broadcast_to(post_ref[2 * slab, k : k + 1], (CY, LANES))
                table1 = jnp.broadcast_to(post_ref[2 * slab + 1, k : k + 1], (CY, LANES))
                for part in range(2):
                    lanes = slice(part * LANES, (part + 1) * LANES)
                    cell = ids[k, :, lanes]
                    low = cell & (LANES - 1)
                    value = jnp.where(cell >= LANES, lane_take(table1, low), lane_take(table0, low))
                    a_ref[slab * CX + x, k, :, lanes] = value

    gates = keep_low, keep_high
    first, second, third = FINE_NODES
    u_copy.wait()
    relax_rows(a_ref, b_ref, 2, 1.0 / PROLONG, *gates, plus=u_ref)
    for k, slab, gate in ((EDGE - 3, 0, keep_low), (EDGE + CX + 2, 2, keep_high)):
        b_ref[k] = (relax(a_ref[k - 1], a_ref[k], a_ref[k + 1], 1.0 / PROLONG) + halo(slab, CX)) * gate
    relax_rows(b_ref, a_ref, 2, first, *gates)
    relax_rows(a_ref, b_ref, 1, second, *gates)
    for x in range(CX):
        k = EDGE + x
        out_ref[:, x] = relax(b_ref[k - 1], b_ref[k], b_ref[k + 1], third) + u_ref[U_EDGE + x]


def call(kernel, out_shape, scratch, flops, scalars=0, spaces=None, hbm_outs=()):
    def spec(k):
        return pl.BlockSpec(memory_space=pltpu.SMEM if k < scalars else (spaces or {}).get(k, pltpu.VMEM))

    single = not isinstance(out_shape, list)
    out_specs = [
        pl.BlockSpec(memory_space=pltpu.HBM if k in hbm_outs else pltpu.VMEM)
        for k in range(1 if single else len(out_shape))
    ]

    def run(*args):
        return pl.pallas_call(
            kernel,
            out_shape=out_shape,
            in_specs=[spec(k) for k in range(len(args))],
            out_specs=out_specs[0] if single else out_specs,
            scratch_shapes=scratch,
            compiler_params=pltpu.CompilerParams(vmem_limit_bytes=24 * 1024 * 1024),
            cost_estimate=pl.CostEstimate(flops=flops, bytes_accessed=2**20, transcendentals=0),
        )(*args)

    return run


def beside(first, second):
    one = [(k, k ^ 1) for k in range(GX)]
    two = [(k, ((k + 1) ^ 1) - 1) for k in range(GX)]
    two = [(k, other % GX) for k, other in two]
    return lax.ppermute(first, "gx", one), lax.ppermute(second, "gx", two)


FINE_FLOPS = 3 * 10**10


def chip_below(value, step):
    return lax.ppermute(value, "gy", [(j, (j + 2 * step) % GY) for j in range(GY)])


def arrived_kernel(low_ref, high_ref, out_ref):
    out_ref[...] = low_ref[0, CX, :, :LANES] + high_ref[0, CX, :, :LANES]


def other_core(value):
    return lax.ppermute(value, "gy", [(j, j ^ 1) for j in range(GY)])


def local(right_side, fine_ids, coarse_diag, coarse_links, coarse_ids, coarsest_inverse):
    row = lax.axis_index("gy")
    place = jnp.stack([lax.axis_index("gx"), row // 2, row % 2]).astype(jnp.int32)
    cells = lax.all_to_all(right_side, "gy", 0, 0, tiled=True)

    arguments = (fine_ids, coarse_diag, coarse_links, coarse_ids)
    tiles = call(
        tiles_kernel,
        pltpu.VMEM((CX + 1, CY, CZ), F32),
        [
            pltpu.VMEM((CX, CY, CZ), jnp.int32),
            pltpu.VMEM((2, 2, 64), F32),
            pltpu.VMEM((6, 2, 2, 64), F32),
            pltpu.VMEM((2, 2, 64), jnp.int32),
            pltpu.SemaphoreType.DMA((4,)),
        ],
        10**8,
        0,
        dict.fromkeys(range(4), pltpu.HBM),
    )(*(pltpu.with_memory_space_constraint(value, pltpu.HBM) for value in arguments))
    slabs = [tiles, *(chip_below(tiles, k) for k in range(1, 4))]
    cells, slabs[3] = lax.optimization_barrier((cells, slabs[3]))
    near = jnp.stack(slabs, axis=0)
    far = other_core(near)

    first, second = beside(cells, cells)

    cells, inverse = lax.optimization_barrier((cells, coarsest_inverse))
    chips = [chip_below(inverse, k) for k in range(1, 4)]

    field = (ROWS, YT, CY, CZ)
    send, *going, u = call(
        down_kernel,
        [
            pltpu.VMEM((GX, 2 + FIELDS, YT, LANES), F32),
            pltpu.VMEM((YT, CX + 1, CY, CZ), F32),
            pltpu.VMEM((YT, CX + 1, CY, CZ), F32),
            pltpu.HBM((CX + 2 * U_EDGE, YT, CY, CZ), F32),
        ],
        [
            pltpu.VMEM(field, F32),
            pltpu.VMEM(field, F32),
            pltpu.VMEM((GY, CY, CZ), F32),
            pltpu.VMEM((CX + 2 * U_EDGE, YT, CY, CZ), F32),
            pltpu.SemaphoreType.DMA,
        ],
        FINE_FLOPS,
        1,
        hbm_outs=(3,),
    )(place, first, cells, second, near, far)
    send, inverse, *chips = lax.optimization_barrier((send, inverse, *chips))
    inverse_near = jnp.stack([inverse, *chips], axis=0)
    inverse_far = other_core(inverse_near)
    first, second = beside(*going)
    got = lax.all_to_all(send, "gx", 0, 0, tiled=True)
    arrived = call(arrived_kernel, pltpu.VMEM((CY, LANES), F32), [], 2 * 10**10)(first, second)
    got, arrived = lax.optimization_barrier((got, arrived))
    send, window, unknowns = call(
        solve_kernel,
        [
            pltpu.VMEM((GX, 1, LANES), F32),
            pltpu.VMEM((10, WINDOW, YT, LANES), F32),
            pltpu.VMEM((WINDOW + 2, YT, LANES), jnp.int32),
        ],
        [pltpu.VMEM((11, NAX, YT, LANES), F32), pltpu.VMEM((LANES, LANES), F32)],
        10**6,
        1,
    )(place, got, other_core(got[:, 2:]), inverse_near, inverse_far, arrived)
    table = lax.all_to_all(send, "gx", 0, 0, tiled=True)
    out = call(
        up_kernel,
        pltpu.VMEM((YT, CX, CY, CZ), F32),
        [
            pltpu.VMEM((6, YT, LANES), F32),
            pltpu.VMEM(field, F32),
            pltpu.VMEM(field, F32),
            pltpu.VMEM((CX + 2 * U_EDGE, YT, CY, CZ), F32),
            pltpu.SemaphoreType.DMA,
        ],
        4 * 10**9,
        1,
        {7: pltpu.HBM},
    )(place, table, window, unknowns, going[0], first, second, pltpu.with_memory_space_constraint(u, pltpu.HBM))
    return lax.all_to_all(out, "gy", 0, 0, tiled=True)


def solution(mesh):
    return jax.shard_map(
        local,
        mesh=mesh,
        in_specs=(
            P(None, "gx", "gy", None),
            P("gx", "gy", None),
            P("gx", "gy", None),
            P(None, "gx", "gy", None),
            P("gx", "gy", None),
            P(("gx", "gy"), None),
        ),
        out_specs=P(None, "gx", "gy", None),
        check_vma=False,
    )
```

```python
import math

import jax
import jax.numpy as jnp
from jax import lax
from jax.experimental import pallas as pl
from jax.experimental.pallas import tpu as pltpu
from jax.sharding import PartitionSpec as P

F32 = jnp.float32
BF16 = jnp.bfloat16

PROLONG = 1.0 / 9.0


def nodes(low, high):
    theta = (high + low) / 2.0
    delta = (high - low) / 2.0
    reach = delta * math.cos(math.pi / 6.0)
    return (theta + reach, theta - reach, theta)


FINE_NODES = tuple(6.0 * node for node in nodes(2.0 / 30.0, 2.0))
COARSE_NODES = nodes(0.19, 1.9)

RHS, CX, YT, CY, CZ = 8, 4, 8, 8, 256
GX, GY = 16, 8
LANES = 128
NC2 = 2048
HI = NC2 // LANES
HALF = LANES // 2


def beside_in_row(row):
    sub = lax.broadcasted_iota(jnp.int32, row.shape, 1)
    lane = lax.broadcasted_iota(jnp.int32, row.shape, 2)
    zero_tile = jnp.zeros((1,) + row.shape[1:], F32)
    up = pltpu.roll(row, 1, 1)
    up = jnp.where(sub == 0, jnp.concatenate([zero_tile, up[:-1]], axis=0), up)
    down = pltpu.roll(row, CY - 1, 1)
    down = jnp.where(sub == CY - 1, jnp.concatenate([down[1:], zero_tile], axis=0), down)
    left = jnp.where(lane == 0, 0.0, pltpu.roll(row, 1, 2))
    right = jnp.where(lane == CZ - 1, 0.0, pltpu.roll(row, CZ - 1, 2))
    return (up + down) + (left + right)


def relax(low, row, high, node):
    return (1.0 - 6.0 / node) * row + (1.0 / node) * (low + high + beside_in_row(row))


def beside_grid(grid):
    sub = lax.broadcasted_iota(jnp.int32, grid.shape, 1)
    lane = lax.broadcasted_iota(jnp.int32, grid.shape, 2)
    turned = pltpu.roll(grid, LANES // 2, 2)
    low_y = jnp.where(lane < LANES // 2, pltpu.roll(turned, 1, 1), turned)
    high_y = jnp.where(lane < LANES // 2, turned, pltpu.roll(turned, YT - 1, 1))
    low_z = pltpu.roll(grid, 1, 2)
    high_z = pltpu.roll(grid, LANES - 1, 2)
    del sub
    return low_y, high_y, low_z, high_z


def lower_of(grid):
    return jnp.concatenate([jnp.zeros((1,) + grid.shape[1:], F32), grid[:-1]], axis=0)


def upper_of(grid):
    return jnp.concatenate([grid[1:], jnp.zeros((1,) + grid.shape[1:], F32)], axis=0)


NAX = 2 * GX
WINDOW = 10
FIELDS = 5


def with_lower(diag, ux, uy, uz):
    return (diag, lower_of(ux), ux, beside_grid(uy)[0], uy, beside_grid(uz)[2], uz, 1.0 / diag)


def coarse_apply(grid, coefs, below=None, above=None):
    diag, lx, ux, ly, uy, lz, uz = coefs[:7]
    low_y, high_y, low_z, high_z = beside_grid(grid)
    low_x = lower_of(grid) if below is None else jnp.concatenate([below[None], grid[:-1]], axis=0)
    high_x = upper_of(grid) if above is None else jnp.concatenate([grid[1:], above[None]], axis=0)
    linked = lx * low_x + ux * high_x
    linked = linked + ly * low_y + uy * high_y
    linked = linked + lz * low_z + uz * high_z
    return diag * grid - linked


def coarse_smooth(residual, coefs, with_last):
    total = None
    for k, node in enumerate(COARSE_NODES):
        update = (1.0 / node) * coefs[7] * residual
        total = update if total is None else total + update
        if k < 2 or with_last:
            residual = residual - coarse_apply(update, coefs)
    return total, residual


def split3(value):
    first = value.astype(BF16)
    rest = value - first.astype(F32)
    second = rest.astype(BF16)
    third = (rest - second.astype(F32)).astype(BF16)
    return first, second, third


def tiles_kernel(
    where_ref, ids_ref, diag_ref, links_ref, coarse_ids_ref, inverse_hbm, out_ref, inverse_ref, id_buf, diag_buf, link_buf, cid_buf, sems
):
    pairs = ((ids_ref, id_buf), (diag_ref, diag_buf), (links_ref, link_buf), (coarse_ids_ref, cid_buf))
    copies = [pltpu.make_async_copy(src, dst, sems.at[k]) for k, (src, dst) in enumerate(pairs)]
    copies.append(pltpu.make_async_copy(inverse_hbm, inverse_ref, sems.at[4]))
    for copy in copies:
        copy.start()
    for copy in copies[:4]:
        copy.wait()
    fields = (
        diag_buf[...],
        link_buf[1],
        link_buf[3],
        link_buf[5],
        cid_buf[...].astype(F32),
    )
    rows = [
        jnp.concatenate([field[half, k : k + 1] for half in range(2) for k in range(2)], axis=1)
        for field in fields
    ]
    rows.append(jnp.zeros((3, CZ), F32))
    for x in range(CX):
        out_ref[x] = id_buf[x].astype(F32)
    out_ref[CX] = jnp.concatenate(rows, axis=0)
    copies[4].wait()


def shared_tile(near_ref, far_ref, chip, core, j, tile):
    k = lax.rem(chip + 4 - j // 2, 4)
    return jnp.where(core == j % 2, near_ref[k, tile], far_ref[k, tile])


def shared_ids(near_ref, far_ref, chip, core, tile):
    rows = [shared_tile(near_ref, far_ref, chip, core, j, tile) for j in range(GY)]
    return jnp.stack(rows, axis=0).astype(jnp.int32)


def pool_matrix():
    lane = lax.broadcasted_iota(jnp.int32, (CZ, LANES), 1)
    gap = lane - lax.broadcasted_iota(jnp.int32, (CZ, LANES), 0) // 4
    parts = []
    for half in range(2):
        for shift in range(-1, 2):
            hit = jnp.logical_and(gap == half * 64 + shift, lane // 64 == half)
            parts.append(jnp.where(hit, 1.0, 0.0).astype(BF16))
    return jnp.concatenate(parts, axis=0)


EDGE = 4
ROWS = CX + 2 * EDGE
U_EDGE = 2


def relax_rows(src, dst, reach, node, keep_low, keep_high, plus=None):
    for k in range(EDGE - reach, EDGE + CX + reach):
        row = relax(src[k - 1], src[k], src[k + 1], node)
        if k < EDGE:
            row = row * keep_low
        elif k >= EDGE + CX:
            row = row * keep_high
        dst[k] = row if plus is None else row + plus[k - EDGE + U_EDGE]


def down_kernel(
    where_ref,
    t1_ref,
    to_ref,
    t2_ref,
    near_ref,
    far_ref,
    send_ref,
    first_ref,
    second_ref,
    u_hbm,
    a_ref,
    b_ref,
    tile_ref,
    u_ref,
    u_sem,
):
    place, chip, core = where_ref[0], where_ref[1], where_ref[2]
    odd = place & 1
    keep_low = jnp.where(place > 0, 1.0, 0.0).astype(F32)
    keep_high = jnp.where(place < GX - 1, 1.0, 0.0).astype(F32)
    gates = keep_low, keep_high
    first, second, third = FINE_NODES
    for x in range(CX):
        a_ref[x] = jnp.where(odd == 1, t1_ref[:, x], t2_ref[:, x]) * keep_low
        a_ref[EDGE + x] = to_ref[:, x]
        a_ref[EDGE + CX + x] = jnp.where(odd == 1, t2_ref[:, x], t1_ref[:, x]) * keep_high

    relax_rows(a_ref, b_ref, 3, first, *gates)
    shift = EDGE - U_EDGE
    for k in range(CX + 2 * U_EDGE):
        u_ref[k] = (1.0 / first) * a_ref[k + shift] + (1.0 / second) * b_ref[k + shift]
    relax_rows(b_ref, a_ref, 2, second, *gates)
    for k in range(CX + 2 * U_EDGE):
        u_ref[k] = u_ref[k] + (1.0 / third) * a_ref[k + shift]
    u_copy = pltpu.make_async_copy(u_ref, u_hbm, u_sem)
    u_copy.start()
    relax_rows(a_ref, b_ref, 1, third, *gates)
    smooth = []
    for x in range(CX):
        k = EDGE + x
        smooth.append(relax(b_ref[k - 1], b_ref[k], b_ref[k + 1], 1.0 / PROLONG))

    shape = (YT, CY, CZ)
    home = lax.broadcasted_iota(jnp.int32, shape, 2) // 4
    codes = []
    for x in range(CX):
        ids = shared_ids(near_ref, far_ref, chip, core, x)
        first_ref[:, x] = ids.astype(F32)
        second_ref[:, x] = ids.astype(F32)
        codes.append((ids >> 6) * 3 + ((ids & 63) - home) + 1)
    first_ref[:, CX] = u_ref[U_EDGE + 1 + odd]
    second_ref[:, CX] = u_ref[U_EDGE + 2 - odd]
    pooled = []
    for half in range(2):
        parts = []
        for k in range(6):
            total = jnp.zeros(shape, F32)
            for x in range(CX):
                total = total + jnp.where(codes[x] == half * 6 + k, smooth[x], 0.0)
            parts.append(jnp.sum(total, axis=1))
        pooled.append(jnp.concatenate(parts, axis=1))
    pooled = jnp.concatenate(pooled, axis=0)
    pieces = jnp.concatenate(split3(pooled)[:2], axis=0)
    sums = jnp.dot(pieces, pool_matrix(), preferred_element_type=F32)
    rows = 2 * YT
    target = sums[:rows] + sums[rows:]
    tiles = [target[:YT], target[YT:]]
    for j in range(GY):
        tile_ref[j] = shared_tile(near_ref, far_ref, chip, core, j, CX)
    halves = [
        tile_ref[:, k, half * LANES : (half + 1) * LANES] for k in range(FIELDS) for half in range(2)
    ]
    for k in range(FIELDS):
        tiles.append(jnp.where(core == 0, halves[k], halves[FIELDS + k]))
    for i in range(GX):
        for k, tile in enumerate(tiles):
            send_ref[i, k] = tile
    u_copy.wait()


def solve_kernel(
    where_ref, got_ref, other_ref, near_ref, far_ref, arrived_ref, send_ref, window_ref, ids_ref, full_ref, total_ref
):
    del arrived_ref

    place, chip, core = where_ref[0], where_ref[1], where_ref[2]

    def grid(k):
        rows = []
        for x in range(NAX):
            side, at = divmod(2 * k + x % 2, FIELDS)
            rows.append(jnp.where(core == side, got_ref[x // 2, 2 + at], other_ref[x // 2, at]))
        return jnp.stack(rows, axis=0)

    coefs = with_lower(grid(0), grid(1), grid(2), grid(3))
    target = jnp.stack([got_ref[x // 2, x % 2] for x in range(NAX)], axis=0)
    pre, residual = coarse_smooth(target, coefs, True)
    for k, value in enumerate((*coefs, pre, residual)):
        full_ref[k] = value
    for k in range(10):
        for w in range(WINDOW):
            x = 2 * place + w - 4
            row = full_ref[k, jnp.clip(x, 0, NAX - 1)]
            if not 4 <= w < 6:
                row = jnp.where(jnp.logical_and(x >= 0, x < NAX), row, 1.0 if k in (0, 7) else 0.0)
            window_ref[k, w] = row
    ids = grid(4)
    full_ref[10] = ids
    for w in range(WINDOW + 2):
        ids_ref[w] = full_ref[10, jnp.clip(2 * place + w - 5, 0, NAX - 1)].astype(jnp.int32)
    ids = ids.astype(jnp.int32)
    high_of = ids >> 6
    low_of = ids & (HALF - 1)
    high_iota = lax.broadcasted_iota(jnp.int32, (NC2 // HALF, LANES), 0)
    low_iota = lax.broadcasted_iota(jnp.int32, (HALF, LANES), 0)
    pieces = [piece.astype(F32) for piece in split3(residual)[:2]]
    counted = jnp.zeros((2 * NC2 // HALF, HALF), F32)
    for x in range(NAX):
        left, right = [], []
        for k in range(YT):
            hit = high_of[x, k : k + 1] == high_iota
            left.append(
                jnp.concatenate([jnp.where(hit, piece[x, k : k + 1], 0.0).astype(BF16) for piece in pieces], axis=0)
            )
            right.append(jnp.where(low_of[x, k : k + 1] == low_iota, 1.0, 0.0).astype(BF16))
        counted = counted + lax.dot_general(
            jnp.concatenate(left, axis=1),
            jnp.concatenate(right, axis=1),
            (((1,), (1,)), ((), ())),
            preferred_element_type=F32,
        )
    rows = NC2 // HALF
    target = sum(counted[k * rows : (k + 1) * rows] for k in range(2))
    target = [jnp.concatenate([target[2 * h : 2 * h + 1], target[2 * h + 1 : 2 * h + 2]], axis=1) for h in range(HI)]
    for ref, side in ((near_ref, core), (far_ref, 1 - core)):
        for k in range(4):
            total = jnp.zeros((HI, LANES), F32)
            for h in range(HI):
                total = total + ref[k, :, h * LANES : (h + 1) * LANES] * target[h]
            at = lax.rem(chip + 4 - k, 4) * 2 + side
            total_ref[pl.ds(pl.multiple_of(at * HI, HI), HI)] = total
    row = jnp.sum(total_ref[...].T, axis=0, keepdims=True)
    for i in range(GX):
        send_ref[i] = row


def lane_take(table, index):
    return jnp.take_along_axis(table, index, axis=1, mode="promise_in_bounds")


def up_kernel(
    where_ref,
    table_ref,
    window_ref,
    ids_ref,
    own_ref,
    first_ref,
    second_ref,
    u_hbm,
    out_ref,
    post_ref,
    a_ref,
    b_ref,
    u_ref,
    u_sem,
):
    u_copy = pltpu.make_async_copy(u_hbm, u_ref, u_sem)
    u_copy.start()
    place = where_ref[0]
    keep_low = jnp.where(place > 0, 1.0, 0.0).astype(F32)
    keep_high = jnp.where(place < GX - 1, 1.0, 0.0).astype(F32)
    coefs = tuple(window_ref[k] for k in range(8))
    picked = []
    for w in range(WINDOW + 2):
        unknown = ids_ref[w]
        high_of = unknown >> 7
        low_of = unknown & (LANES - 1)
        value = jnp.zeros((YT, LANES), F32)
        for k in range(HI):
            table = jnp.broadcast_to(table_ref[k], (YT, LANES))
            value = jnp.where(high_of == k, lane_take(table, low_of), value)
        picked.append(value)
    coarsest = jnp.stack(picked[1:-1], axis=0)
    rest = window_ref[9] - coarse_apply(coarsest, coefs, picked[0], picked[-1])
    update, unused = coarse_smooth(rest, coefs, False)
    post = window_ref[8] + coarsest + update
    for k in range(6):
        gate = keep_low if k < 2 else (keep_high if k >= 4 else None)
        row = post[k + 2]
        post_ref[k] = row if gate is None else row * gate

    odd = place & 1

    def halo(slab, x):
        first, second = first_ref[:, x], second_ref[:, x]
        return jnp.where(odd == 1, first, second) if slab == 0 else jnp.where(odd == 1, second, first)

    for slab in range(3):
        for x in range(CX):
            ids = (own_ref[:, x] if slab == 1 else halo(slab, x)).astype(jnp.int32)
            for k in range(YT):
                table0 = jnp.broadcast_to(post_ref[2 * slab, k : k + 1], (CY, LANES))
                table1 = jnp.broadcast_to(post_ref[2 * slab + 1, k : k + 1], (CY, LANES))
                for part in range(2):
                    lanes = slice(part * LANES, (part + 1) * LANES)
                    cell = ids[k, :, lanes]
                    low = cell & (LANES - 1)
                    value = jnp.where(cell >= LANES, lane_take(table1, low), lane_take(table0, low))
                    a_ref[slab * CX + x, k, :, lanes] = value

    gates = keep_low, keep_high
    first, second, third = FINE_NODES
    u_copy.wait()
    relax_rows(a_ref, b_ref, 2, 1.0 / PROLONG, *gates, plus=u_ref)
    for k, slab, gate in ((EDGE - 3, 0, keep_low), (EDGE + CX + 2, 2, keep_high)):
        b_ref[k] = (relax(a_ref[k - 1], a_ref[k], a_ref[k + 1], 1.0 / PROLONG) + halo(slab, CX)) * gate
    relax_rows(b_ref, a_ref, 2, first, *gates)
    relax_rows(a_ref, b_ref, 1, second, *gates)
    for x in range(CX):
        k = EDGE + x
        out_ref[:, x] = relax(b_ref[k - 1], b_ref[k], b_ref[k + 1], third) + u_ref[U_EDGE + x]


def call(kernel, out_shape, scratch, flops, scalars=0, spaces=None, hbm_outs=()):
    def spec(k):
        return pl.BlockSpec(memory_space=pltpu.SMEM if k < scalars else (spaces or {}).get(k, pltpu.VMEM))

    single = not isinstance(out_shape, list)
    out_specs = [
        pl.BlockSpec(memory_space=pltpu.HBM if k in hbm_outs else pltpu.VMEM)
        for k in range(1 if single else len(out_shape))
    ]

    def run(*args):
        return pl.pallas_call(
            kernel,
            out_shape=out_shape,
            in_specs=[spec(k) for k in range(len(args))],
            out_specs=out_specs[0] if single else out_specs,
            scratch_shapes=scratch,
            compiler_params=pltpu.CompilerParams(vmem_limit_bytes=24 * 1024 * 1024),
            cost_estimate=pl.CostEstimate(flops=flops, bytes_accessed=2**20, transcendentals=0),
        )(*args)

    return run


def beside(first, second):
    one = [(k, k ^ 1) for k in range(GX)]
    two = [(k, ((k + 1) ^ 1) - 1) for k in range(GX)]
    two = [(k, other % GX) for k, other in two]
    return lax.ppermute(first, "gx", one), lax.ppermute(second, "gx", two)


FINE_FLOPS = 3 * 10**10


def chip_below(value, step):
    return lax.ppermute(value, "gy", [(j, (j + 2 * step) % GY) for j in range(GY)])


def arrived_kernel(low_ref, high_ref, out_ref):
    out_ref[...] = low_ref[0, CX, :, :LANES] + high_ref[0, CX, :, :LANES]


def other_core(value):
    return lax.ppermute(value, "gy", [(j, j ^ 1) for j in range(GY)])


def local(right_side, fine_ids, coarse_diag, coarse_links, coarse_ids, coarsest_inverse):
    row = lax.axis_index("gy")
    place = jnp.stack([lax.axis_index("gx"), row // 2, row % 2]).astype(jnp.int32)
    cells = lax.all_to_all(right_side, "gy", 0, 0, tiled=True)

    arguments = (fine_ids, coarse_diag, coarse_links, coarse_ids, coarsest_inverse)
    tiles, inverse = call(
        tiles_kernel,
        [pltpu.VMEM((CX + 1, CY, CZ), F32), pltpu.VMEM((HI, NC2), F32)],
        [
            pltpu.VMEM((CX, CY, CZ), jnp.int32),
            pltpu.VMEM((2, 2, 64), F32),
            pltpu.VMEM((6, 2, 2, 64), F32),
            pltpu.VMEM((2, 2, 64), jnp.int32),
            pltpu.SemaphoreType.DMA((5,)),
        ],
        10**8,
        1,
        dict.fromkeys(range(1, 6), pltpu.HBM),
    )(place, *(pltpu.with_memory_space_constraint(value, pltpu.HBM) for value in arguments))
    slabs = [tiles, *(chip_below(tiles, k) for k in range(1, 4))]
    cells, slabs[3] = lax.optimization_barrier((cells, slabs[3]))
    near = jnp.stack(slabs, axis=0)
    far = other_core(near)

    first, second = beside(cells, cells)

    cells, inverse = lax.optimization_barrier((cells, inverse))
    chips = [chip_below(inverse, k) for k in range(1, 4)]

    field = (ROWS, YT, CY, CZ)
    send, *going, u = call(
        down_kernel,
        [
            pltpu.VMEM((GX, 2 + FIELDS, YT, LANES), F32),
            pltpu.VMEM((YT, CX + 1, CY, CZ), F32),
            pltpu.VMEM((YT, CX + 1, CY, CZ), F32),
            pltpu.HBM((CX + 2 * U_EDGE, YT, CY, CZ), F32),
        ],
        [
            pltpu.VMEM(field, F32),
            pltpu.VMEM(field, F32),
            pltpu.VMEM((GY, CY, CZ), F32),
            pltpu.VMEM((CX + 2 * U_EDGE, YT, CY, CZ), F32),
            pltpu.SemaphoreType.DMA,
        ],
        FINE_FLOPS,
        1,
        hbm_outs=(3,),
    )(place, first, cells, second, near, far)
    send, chips[0], chips[2] = lax.optimization_barrier((send, chips[0], chips[2]))
    inverse_near = jnp.stack([inverse, *chips], axis=0)
    inverse_far = other_core(inverse_near)
    first, second = beside(*going)
    got = lax.all_to_all(send, "gx", 0, 0, tiled=True)
    arrived = call(arrived_kernel, pltpu.VMEM((CY, LANES), F32), [], 2 * 10**10)(first, second)
    got, arrived = lax.optimization_barrier((got, arrived))
    send, window, unknowns = call(
        solve_kernel,
        [
            pltpu.VMEM((GX, 1, LANES), F32),
            pltpu.VMEM((10, WINDOW, YT, LANES), F32),
            pltpu.VMEM((WINDOW + 2, YT, LANES), jnp.int32),
        ],
        [pltpu.VMEM((11, NAX, YT, LANES), F32), pltpu.VMEM((LANES, LANES), F32)],
        10**6,
        1,
    )(place, got, other_core(got[:, 2:]), inverse_near, inverse_far, arrived)
    table = lax.all_to_all(send, "gx", 0, 0, tiled=True)
    out = call(
        up_kernel,
        pltpu.VMEM((YT, CX, CY, CZ), F32),
        [
            pltpu.VMEM((6, YT, LANES), F32),
            pltpu.VMEM(field, F32),
            pltpu.VMEM(field, F32),
            pltpu.VMEM((CX + 2 * U_EDGE, YT, CY, CZ), F32),
            pltpu.SemaphoreType.DMA,
        ],
        4 * 10**9,
        1,
        {7: pltpu.HBM},
    )(place, table, window, unknowns, going[0], first, second, pltpu.with_memory_space_constraint(u, pltpu.HBM))
    return lax.all_to_all(out, "gy", 0, 0, tiled=True)


def solution(mesh):
    return jax.shard_map(
        local,
        mesh=mesh,
        in_specs=(
            P(None, "gx", "gy", None),
            P("gx", "gy", None),
            P("gx", "gy", None),
            P(None, "gx", "gy", None),
            P("gx", "gy", None),
            P(("gx", "gy"), None),
        ),
        out_specs=P(None, "gx", "gy", None),
        check_vma=False,
    )
```

```python
import math

import jax
import jax.numpy as jnp
from jax import lax
from jax.experimental import pallas as pl
from jax.experimental.pallas import tpu as pltpu
from jax.sharding import PartitionSpec as P

F32 = jnp.float32
BF16 = jnp.bfloat16

PROLONG = 1.0 / 9.0


def nodes(low, high):
    theta = (high + low) / 2.0
    delta = (high - low) / 2.0
    reach = delta * math.cos(math.pi / 6.0)
    return (theta + reach, theta - reach, theta)


FINE_NODES = tuple(6.0 * node for node in nodes(2.0 / 30.0, 2.0))
COARSE_NODES = nodes(0.19, 1.9)

RHS, CX, YT, CY, CZ = 8, 4, 8, 8, 256
GX, GY = 16, 8
LANES = 128
NC2 = 2048
HI = NC2 // LANES
HALF = LANES // 2


def beside_in_row(row):
    sub = lax.broadcasted_iota(jnp.int32, row.shape, 1)
    lane = lax.broadcasted_iota(jnp.int32, row.shape, 2)
    zero_tile = jnp.zeros((1,) + row.shape[1:], F32)
    up = pltpu.roll(row, 1, 1)
    up = jnp.where(sub == 0, jnp.concatenate([zero_tile, up[:-1]], axis=0), up)
    down = pltpu.roll(row, CY - 1, 1)
    down = jnp.where(sub == CY - 1, jnp.concatenate([down[1:], zero_tile], axis=0), down)
    left = jnp.where(lane == 0, 0.0, pltpu.roll(row, 1, 2))
    right = jnp.where(lane == CZ - 1, 0.0, pltpu.roll(row, CZ - 1, 2))
    return (up + down) + (left + right)


def relax(low, row, high, node):
    return (1.0 - 6.0 / node) * row + (1.0 / node) * (low + high + beside_in_row(row))


def beside_grid(grid):
    sub = lax.broadcasted_iota(jnp.int32, grid.shape, 1)
    lane = lax.broadcasted_iota(jnp.int32, grid.shape, 2)
    turned = pltpu.roll(grid, LANES // 2, 2)
    low_y = jnp.where(lane < LANES // 2, pltpu.roll(turned, 1, 1), turned)
    high_y = jnp.where(lane < LANES // 2, turned, pltpu.roll(turned, YT - 1, 1))
    low_z = pltpu.roll(grid, 1, 2)
    high_z = pltpu.roll(grid, LANES - 1, 2)
    del sub
    return low_y, high_y, low_z, high_z


def lower_of(grid):
    return jnp.concatenate([jnp.zeros((1,) + grid.shape[1:], F32), grid[:-1]], axis=0)


def upper_of(grid):
    return jnp.concatenate([grid[1:], jnp.zeros((1,) + grid.shape[1:], F32)], axis=0)


NAX = 2 * GX
WINDOW = 10
FIELDS = 5


def with_lower(diag, ux, uy, uz):
    return (diag, lower_of(ux), ux, beside_grid(uy)[0], uy, beside_grid(uz)[2], uz, 1.0 / diag)


def coarse_apply(grid, coefs, below=None, above=None):
    diag, lx, ux, ly, uy, lz, uz = coefs[:7]
    low_y, high_y, low_z, high_z = beside_grid(grid)
    low_x = lower_of(grid) if below is None else jnp.concatenate([below[None], grid[:-1]], axis=0)
    high_x = upper_of(grid) if above is None else jnp.concatenate([grid[1:], above[None]], axis=0)
    linked = lx * low_x + ux * high_x
    linked = linked + ly * low_y + uy * high_y
    linked = linked + lz * low_z + uz * high_z
    return diag * grid - linked


def coarse_smooth(residual, coefs, with_last):
    total = None
    for k, node in enumerate(COARSE_NODES):
        update = (1.0 / node) * coefs[7] * residual
        total = update if total is None else total + update
        if k < 2 or with_last:
            residual = residual - coarse_apply(update, coefs)
    return total, residual


def split3(value):
    first = value.astype(BF16)
    rest = value - first.astype(F32)
    second = rest.astype(BF16)
    third = (rest - second.astype(F32)).astype(BF16)
    return first, second, third


def tiles_kernel(
    where_ref, ids_ref, diag_ref, links_ref, coarse_ids_ref, inverse_hbm, out_ref, inverse_ref, id_buf, diag_buf, link_buf, cid_buf, sems
):
    pairs = ((ids_ref, id_buf), (diag_ref, diag_buf), (links_ref, link_buf), (coarse_ids_ref, cid_buf))
    copies = [pltpu.make_async_copy(src, dst, sems.at[k]) for k, (src, dst) in enumerate(pairs)]
    copies.append(pltpu.make_async_copy(inverse_hbm, inverse_ref, sems.at[4]))
    for copy in copies:
        copy.start()
    for copy in copies[:4]:
        copy.wait()
    fields = (
        diag_buf[...],
        link_buf[1],
        link_buf[3],
        link_buf[5],
        cid_buf[...].astype(F32),
    )
    rows = [
        jnp.concatenate([field[half, k : k + 1] for half in range(2) for k in range(2)], axis=1)
        for field in fields
    ]
    rows.append(jnp.zeros((3, CZ), F32))
    for x in range(CX):
        out_ref[x] = id_buf[x].astype(F32)
    out_ref[CX] = jnp.concatenate(rows, axis=0)
    copies[4].wait()


def shared_tile(near_ref, far_ref, chip, core, j, tile):
    k = lax.rem(chip + 4 - j // 2, 4)
    return jnp.where(core == j % 2, near_ref[k, tile], far_ref[k, tile])


def shared_ids(near_ref, far_ref, chip, core, tile):
    rows = [shared_tile(near_ref, far_ref, chip, core, j, tile) for j in range(GY)]
    return jnp.stack(rows, axis=0).astype(jnp.int32)


def pool_matrix():
    lane = lax.broadcasted_iota(jnp.int32, (CZ, LANES), 1)
    gap = lane - lax.broadcasted_iota(jnp.int32, (CZ, LANES), 0) // 4
    parts = []
    for half in range(2):
        for shift in range(-1, 2):
            hit = jnp.logical_and(gap == half * 64 + shift, lane // 64 == half)
            parts.append(jnp.where(hit, 1.0, 0.0).astype(BF16))
    return jnp.concatenate(parts, axis=0)


EDGE = 4
ROWS = CX + 2 * EDGE
U_EDGE = 2


def relax_rows(src, dst, reach, node, keep_low, keep_high, plus=None):
    for k in range(EDGE - reach, EDGE + CX + reach):
        row = relax(src[k - 1], src[k], src[k + 1], node)
        if k < EDGE:
            row = row * keep_low
        elif k >= EDGE + CX:
            row = row * keep_high
        dst[k] = row if plus is None else row + plus[k - EDGE + U_EDGE]


def down_kernel(
    where_ref,
    t1_ref,
    to_ref,
    t2_ref,
    near_ref,
    far_ref,
    send_ref,
    first_ref,
    second_ref,
    u_hbm,
    a_ref,
    b_ref,
    tile_ref,
    u_ref,
    u_sem,
):
    place, chip, core = where_ref[0], where_ref[1], where_ref[2]
    odd = place & 1
    keep_low = jnp.where(place > 0, 1.0, 0.0).astype(F32)
    keep_high = jnp.where(place < GX - 1, 1.0, 0.0).astype(F32)
    gates = keep_low, keep_high
    first, second, third = FINE_NODES
    for x in range(CX):
        a_ref[x] = jnp.where(odd == 1, t1_ref[:, x], t2_ref[:, x]) * keep_low
        a_ref[EDGE + x] = to_ref[:, x]
        a_ref[EDGE + CX + x] = jnp.where(odd == 1, t2_ref[:, x], t1_ref[:, x]) * keep_high

    relax_rows(a_ref, b_ref, 3, first, *gates)
    shift = EDGE - U_EDGE
    for k in range(CX + 2 * U_EDGE):
        u_ref[k] = (1.0 / first) * a_ref[k + shift] + (1.0 / second) * b_ref[k + shift]
    relax_rows(b_ref, a_ref, 2, second, *gates)
    for k in range(CX + 2 * U_EDGE):
        u_ref[k] = u_ref[k] + (1.0 / third) * a_ref[k + shift]
    u_copy = pltpu.make_async_copy(u_ref, u_hbm, u_sem)
    u_copy.start()
    relax_rows(a_ref, b_ref, 1, third, *gates)
    smooth = []
    for x in range(CX):
        k = EDGE + x
        smooth.append(relax(b_ref[k - 1], b_ref[k], b_ref[k + 1], 1.0 / PROLONG))

    shape = (YT, CY, CZ)
    home = lax.broadcasted_iota(jnp.int32, shape, 2) // 4
    codes = []
    for x in range(CX):
        ids = shared_ids(near_ref, far_ref, chip, core, x)
        first_ref[:, x] = ids.astype(F32)
        second_ref[:, x] = ids.astype(F32)
        codes.append((ids >> 6) * 3 + ((ids & 63) - home) + 1)
    first_ref[:, CX] = u_ref[U_EDGE + 1 + odd]
    second_ref[:, CX] = u_ref[U_EDGE + 2 - odd]
    pooled = []
    for half in range(2):
        parts = []
        for k in range(6):
            total = jnp.zeros(shape, F32)
            for x in range(CX):
                total = total + jnp.where(codes[x] == half * 6 + k, smooth[x], 0.0)
            parts.append(jnp.sum(total, axis=1))
        pooled.append(jnp.concatenate(parts, axis=1))
    pooled = jnp.concatenate(pooled, axis=0)
    pieces = jnp.concatenate(split3(pooled)[:2], axis=0)
    sums = jnp.dot(pieces, pool_matrix(), preferred_element_type=F32)
    rows = 2 * YT
    target = sums[:rows] + sums[rows:]
    tiles = [target[:YT], target[YT:]]
    for j in range(GY):
        tile_ref[j] = shared_tile(near_ref, far_ref, chip, core, j, CX)
    halves = [
        tile_ref[:, k, half * LANES : (half + 1) * LANES] for k in range(FIELDS) for half in range(2)
    ]
    for k in range(FIELDS):
        tiles.append(jnp.where(core == 0, halves[k], halves[FIELDS + k]))
    for i in range(GX):
        for k, tile in enumerate(tiles):
            send_ref[i, k] = tile
    u_copy.wait()


def solve_kernel(
    where_ref, got_ref, other_ref, near_ref, far_ref, arrived_ref, send_ref, window_ref, ids_ref, full_ref, total_ref
):
    del arrived_ref

    place, chip, core = where_ref[0], where_ref[1], where_ref[2]

    def grid(k):
        rows = []
        for x in range(NAX):
            side, at = divmod(2 * k + x % 2, FIELDS)
            rows.append(jnp.where(core == side, got_ref[x // 2, 2 + at], other_ref[x // 2, at]))
        return jnp.stack(rows, axis=0)

    coefs = with_lower(grid(0), grid(1), grid(2), grid(3))
    target = jnp.stack([got_ref[x // 2, x % 2] for x in range(NAX)], axis=0)
    pre, residual = coarse_smooth(target, coefs, True)
    for k, value in enumerate((*coefs, pre, residual)):
        full_ref[k] = value
    for k in range(10):
        for w in range(WINDOW):
            x = 2 * place + w - 4
            row = full_ref[k, jnp.clip(x, 0, NAX - 1)]
            if not 4 <= w < 6:
                row = jnp.where(jnp.logical_and(x >= 0, x < NAX), row, 1.0 if k in (0, 7) else 0.0)
            window_ref[k, w] = row
    ids = grid(4)
    full_ref[10] = ids
    for w in range(WINDOW + 2):
        ids_ref[w] = full_ref[10, jnp.clip(2 * place + w - 5, 0, NAX - 1)].astype(jnp.int32)
    ids = ids.astype(jnp.int32)
    high_of = ids >> 6
    low_of = ids & (HALF - 1)
    high_iota = lax.broadcasted_iota(jnp.int32, (NC2 // HALF, LANES), 0)
    low_iota = lax.broadcasted_iota(jnp.int32, (HALF, LANES), 0)
    pieces = [piece.astype(F32) for piece in split3(residual)[:2]]
    counted = jnp.zeros((2 * NC2 // HALF, HALF), F32)
    for start in range(0, NAX, 4):
        left, right = [], []
        for x, k in [(x, k) for x in range(start, start + 4) for k in range(YT)]:
            hit = high_of[x, k : k + 1] == high_iota
            left.append(
                jnp.concatenate([jnp.where(hit, piece[x, k : k + 1], 0.0).astype(BF16) for piece in pieces], axis=0)
            )
            right.append(jnp.where(low_of[x, k : k + 1] == low_iota, 1.0, 0.0).astype(BF16))
        counted = counted + lax.dot_general(
            jnp.concatenate(left, axis=1),
            jnp.concatenate(right, axis=1),
            (((1,), (1,)), ((), ())),
            preferred_element_type=F32,
        )
    rows = NC2 // HALF
    target = sum(counted[k * rows : (k + 1) * rows] for k in range(2))
    target = [jnp.concatenate([target[2 * h : 2 * h + 1], target[2 * h + 1 : 2 * h + 2]], axis=1) for h in range(HI)]
    for ref, side in ((near_ref, core), (far_ref, 1 - core)):
        for k in range(4):
            total = jnp.zeros((HI, LANES), F32)
            for h in range(HI):
                total = total + ref[k, :, h * LANES : (h + 1) * LANES] * target[h]
            at = lax.rem(chip + 4 - k, 4) * 2 + side
            total_ref[pl.ds(pl.multiple_of(at * HI, HI), HI)] = total
    row = jnp.sum(total_ref[...].T, axis=0, keepdims=True)
    for i in range(GX):
        send_ref[i] = row


def lane_take(table, index):
    return jnp.take_along_axis(table, index, axis=1, mode="promise_in_bounds")


def up_kernel(
    where_ref,
    table_ref,
    window_ref,
    ids_ref,
    own_ref,
    first_ref,
    second_ref,
    u_hbm,
    out_ref,
    post_ref,
    a_ref,
    b_ref,
    u_ref,
    u_sem,
):
    u_copy = pltpu.make_async_copy(u_hbm, u_ref, u_sem)
    u_copy.start()
    place = where_ref[0]
    keep_low = jnp.where(place > 0, 1.0, 0.0).astype(F32)
    keep_high = jnp.where(place < GX - 1, 1.0, 0.0).astype(F32)
    coefs = tuple(window_ref[k] for k in range(8))
    picked = []
    for w in range(WINDOW + 2):
        unknown = ids_ref[w]
        high_of = unknown >> 7
        low_of = unknown & (LANES - 1)
        value = jnp.zeros((YT, LANES), F32)
        for k in range(HI):
            table = jnp.broadcast_to(table_ref[k], (YT, LANES))
            value = jnp.where(high_of == k, lane_take(table, low_of), value)
        picked.append(value)
    coarsest = jnp.stack(picked[1:-1], axis=0)
    rest = window_ref[9] - coarse_apply(coarsest, coefs, picked[0], picked[-1])
    update, unused = coarse_smooth(rest, coefs, False)
    post = window_ref[8] + coarsest + update
    for k in range(6):
        gate = keep_low if k < 2 else (keep_high if k >= 4 else None)
        row = post[k + 2]
        post_ref[k] = row if gate is None else row * gate

    odd = place & 1

    def halo(slab, x):
        first, second = first_ref[:, x], second_ref[:, x]
        return jnp.where(odd == 1, first, second) if slab == 0 else jnp.where(odd == 1, second, first)

    for slab in range(3):
        for x in range(CX):
            ids = (own_ref[:, x] if slab == 1 else halo(slab, x)).astype(jnp.int32)
            for k in range(YT):
                table0 = jnp.broadcast_to(post_ref[2 * slab, k : k + 1], (CY, LANES))
                table1 = jnp.broadcast_to(post_ref[2 * slab + 1, k : k + 1], (CY, LANES))
                for part in range(2):
                    lanes = slice(part * LANES, (part + 1) * LANES)
                    cell = ids[k, :, lanes]
                    low = cell & (LANES - 1)
                    value = jnp.where(cell >= LANES, lane_take(table1, low), lane_take(table0, low))
                    a_ref[slab * CX + x, k, :, lanes] = value

    gates = keep_low, keep_high
    first, second, third = FINE_NODES
    u_copy.wait()
    relax_rows(a_ref, b_ref, 2, 1.0 / PROLONG, *gates, plus=u_ref)
    for k, slab, gate in ((EDGE - 3, 0, keep_low), (EDGE + CX + 2, 2, keep_high)):
        b_ref[k] = (relax(a_ref[k - 1], a_ref[k], a_ref[k + 1], 1.0 / PROLONG) + halo(slab, CX)) * gate
    relax_rows(b_ref, a_ref, 2, first, *gates)
    relax_rows(a_ref, b_ref, 1, second, *gates)
    for x in range(CX):
        k = EDGE + x
        out_ref[:, x] = relax(b_ref[k - 1], b_ref[k], b_ref[k + 1], third) + u_ref[U_EDGE + x]


def call(kernel, out_shape, scratch, flops, scalars=0, spaces=None, hbm_outs=()):
    def spec(k):
        return pl.BlockSpec(memory_space=pltpu.SMEM if k < scalars else (spaces or {}).get(k, pltpu.VMEM))

    single = not isinstance(out_shape, list)
    out_specs = [
        pl.BlockSpec(memory_space=pltpu.HBM if k in hbm_outs else pltpu.VMEM)
        for k in range(1 if single else len(out_shape))
    ]

    def run(*args):
        return pl.pallas_call(
            kernel,
            out_shape=out_shape,
            in_specs=[spec(k) for k in range(len(args))],
            out_specs=out_specs[0] if single else out_specs,
            scratch_shapes=scratch,
            compiler_params=pltpu.CompilerParams(vmem_limit_bytes=24 * 1024 * 1024),
            cost_estimate=pl.CostEstimate(flops=flops, bytes_accessed=2**20, transcendentals=0),
        )(*args)

    return run


def beside(first, second):
    one = [(k, k ^ 1) for k in range(GX)]
    two = [(k, ((k + 1) ^ 1) - 1) for k in range(GX)]
    two = [(k, other % GX) for k, other in two]
    return lax.ppermute(first, "gx", one), lax.ppermute(second, "gx", two)


FINE_FLOPS = 3 * 10**10


def chip_below(value, step):
    return lax.ppermute(value, "gy", [(j, (j + 2 * step) % GY) for j in range(GY)])


def arrived_kernel(low_ref, high_ref, out_ref):
    out_ref[...] = low_ref[0, CX, :, :LANES] + high_ref[0, CX, :, :LANES]


def other_core(value):
    return lax.ppermute(value, "gy", [(j, j ^ 1) for j in range(GY)])


def local(right_side, fine_ids, coarse_diag, coarse_links, coarse_ids, coarsest_inverse):
    row = lax.axis_index("gy")
    place = jnp.stack([lax.axis_index("gx"), row // 2, row % 2]).astype(jnp.int32)
    cells = lax.all_to_all(right_side, "gy", 0, 0, tiled=True)

    arguments = (fine_ids, coarse_diag, coarse_links, coarse_ids, coarsest_inverse)
    tiles, inverse = call(
        tiles_kernel,
        [pltpu.VMEM((CX + 1, CY, CZ), F32), pltpu.VMEM((HI, NC2), F32)],
        [
            pltpu.VMEM((CX, CY, CZ), jnp.int32),
            pltpu.VMEM((2, 2, 64), F32),
            pltpu.VMEM((6, 2, 2, 64), F32),
            pltpu.VMEM((2, 2, 64), jnp.int32),
            pltpu.SemaphoreType.DMA((5,)),
        ],
        10**8,
        1,
        dict.fromkeys(range(1, 6), pltpu.HBM),
    )(place, *(pltpu.with_memory_space_constraint(value, pltpu.HBM) for value in arguments))
    slabs = [tiles, *(chip_below(tiles, k) for k in range(1, 4))]
    cells, slabs[3] = lax.optimization_barrier((cells, slabs[3]))
    near = jnp.stack(slabs, axis=0)
    far = other_core(near)

    first, second = beside(cells, cells)

    cells, inverse = lax.optimization_barrier((cells, inverse))
    chips = [chip_below(inverse, k) for k in range(1, 4)]

    field = (ROWS, YT, CY, CZ)
    send, *going, u = call(
        down_kernel,
        [
            pltpu.VMEM((GX, 2 + FIELDS, YT, LANES), F32),
            pltpu.VMEM((YT, CX + 1, CY, CZ), F32),
            pltpu.VMEM((YT, CX + 1, CY, CZ), F32),
            pltpu.HBM((CX + 2 * U_EDGE, YT, CY, CZ), F32),
        ],
        [
            pltpu.VMEM(field, F32),
            pltpu.VMEM(field, F32),
            pltpu.VMEM((GY, CY, CZ), F32),
            pltpu.VMEM((CX + 2 * U_EDGE, YT, CY, CZ), F32),
            pltpu.SemaphoreType.DMA,
        ],
        FINE_FLOPS,
        1,
        hbm_outs=(3,),
    )(place, first, cells, second, near, far)
    send, chips[0], chips[2] = lax.optimization_barrier((send, chips[0], chips[2]))
    inverse_near = jnp.stack([inverse, *chips], axis=0)
    inverse_far = other_core(inverse_near)
    first, second = beside(*going)
    got = lax.all_to_all(send, "gx", 0, 0, tiled=True)
    arrived = call(arrived_kernel, pltpu.VMEM((CY, LANES), F32), [], 2 * 10**10)(first, second)
    got, arrived = lax.optimization_barrier((got, arrived))
    send, window, unknowns = call(
        solve_kernel,
        [
            pltpu.VMEM((GX, 1, LANES), F32),
            pltpu.VMEM((10, WINDOW, YT, LANES), F32),
            pltpu.VMEM((WINDOW + 2, YT, LANES), jnp.int32),
        ],
        [pltpu.VMEM((11, NAX, YT, LANES), F32), pltpu.VMEM((LANES, LANES), F32)],
        10**6,
        1,
    )(place, got, other_core(got[:, 2:]), inverse_near, inverse_far, arrived)
    table = lax.all_to_all(send, "gx", 0, 0, tiled=True)
    out = call(
        up_kernel,
        pltpu.VMEM((YT, CX, CY, CZ), F32),
        [
            pltpu.VMEM((6, YT, LANES), F32),
            pltpu.VMEM(field, F32),
            pltpu.VMEM(field, F32),
            pltpu.VMEM((CX + 2 * U_EDGE, YT, CY, CZ), F32),
            pltpu.SemaphoreType.DMA,
        ],
        4 * 10**9,
        1,
        {7: pltpu.HBM},
    )(place, table, window, unknowns, going[0], first, second, pltpu.with_memory_space_constraint(u, pltpu.HBM))
    return lax.all_to_all(out, "gy", 0, 0, tiled=True)


def solution(mesh):
    return jax.shard_map(
        local,
        mesh=mesh,
        in_specs=(
            P(None, "gx", "gy", None),
            P("gx", "gy", None),
            P("gx", "gy", None),
            P(None, "gx", "gy", None),
            P("gx", "gy", None),
            P(("gx", "gy"), None),
        ),
        out_specs=P(None, "gx", "gy", None),
        check_vma=False,
    )
```
